512 devices in a mesh: gx: 16 (over z), gy: 8 (over x, core), gz: 4 (over y).
Axes of the slice: x: 4, y: 4, z: 16, core: 2. Of those that a mesh axis runs over, the one named last changes fastest.
Arguments:
- field: float32 [2, 256, 512, 512], P(None, 'gx', 'gy', 'gz'), may hold values from -24 to 24
Outputs:
- core: float32 [2, 256, 512, 128], P(None, 'gx', ('gy', 'gz'))
- factor: float32 [512, 128], replicated
The draws below stay inside these ranges and needn't reach their ends.
All inputs are finite; a program needn't handle non-finite values.
Results may differ from the reference program's by a relative error of at most 0.0003.
Values sent between devices are 32-bit elements; how exact they have to be, the bound alone decides.
A program may use at most 64 MiB of HBM per device.

```python
import math
import jax
import jax.numpy as jnp
from jax import lax

STEPS = 2
NZ = 512
RANK = 128
ITERS = 4
NX = 256
NY = 512


def draw_field(key, part):
    key = jax.random.fold_in(key, 11)
    k_noise, k_amps, k_freqs, k_phases, k_scales = jax.random.split(key, 5)
    noise = jnp.clip(jax.random.normal(k_noise, (STEPS, NX, NY, NZ), jnp.float32), -4.0, 4.0)
    amps = jnp.clip(jax.random.normal(k_amps, (2, STEPS, NX, NY, 1), jnp.float32), -3.0, 3.0)
    freqs = jax.random.uniform(k_freqs, (2, STEPS, NX, NY, 1), jnp.float32, 0.0, 1.3)
    phases = jax.random.uniform(k_phases, (2, STEPS, NX, NY, 1), jnp.float32, -math.pi, math.pi)
    depth = (jnp.arange(NZ, dtype=jnp.float32) - jnp.float32(NZ // 2)).reshape(1, 1, 1, NZ)
    waves = amps[0] * jnp.cos(freqs[0] * depth + phases[0]) + amps[1] * jnp.cos(freqs[1] * depth + phases[1])
    scales = jnp.exp(jax.random.uniform(k_scales, (1, 1, 1, NZ), jnp.float32, 0.0, math.log(4.0)))
    ramp = 1.0 + 2.0 * jnp.arange(NX, dtype=jnp.float32).reshape(1, NX, 1, 1) / max(NX - 1, 1)
    values = ramp * scales * (noise + waves) / 4.0
    return jnp.clip(values, -24.0, 24.0).astype(jnp.float32)


def setup_inputs(seed: int = 0) -> dict:
    key_of = jax.random.split(jax.random.key(seed), 2)
    return {
        "field": draw_field(jax.random.fold_in(key_of[1], 71), 0),
    }


def orthogonal_steps(gram):
    factor = jnp.eye(NZ, RANK, dtype=jnp.float32)
    for step in range(ITERS):
        grown = jnp.dot(gram.astype(jnp.float32), factor.astype(jnp.float32), precision=lax.Precision.HIGHEST, preferred_element_type=jnp.float32)
        inner = jnp.dot(grown.T.astype(jnp.float32), grown.astype(jnp.float32), precision=lax.Precision.HIGHEST, preferred_element_type=jnp.float32)
        lower = jnp.linalg.cholesky(inner)
        factor = lax.linalg.triangular_solve(lower, grown, left_side=False, lower=True, transpose_a=True)
    return factor

def reference(field):
    fibres = field.reshape(-1, NZ)
    gram = lax.dot_general(fibres.astype(jnp.float32), fibres.astype(jnp.float32), (((0,), (0,)), ((), ())), precision=lax.Precision.HIGHEST, preferred_element_type=jnp.float32)
    gram = gram / jnp.float32(STEPS * NX * NY)
    factor = orthogonal_steps(gram)
    core = jnp.dot(fibres.astype(jnp.float32), factor.astype(jnp.float32), precision=lax.Precision.HIGHEST, preferred_element_type=jnp.float32)
    return (core.reshape(STEPS, NX, NY, RANK), factor)
```

```python
import functools

import jax
import jax.numpy as jnp
from jax import lax
from jax.experimental import pallas as pl
from jax.experimental.pallas import tpu as pltpu
from jax.sharding import PartitionSpec as P

RANK = 128
ITERS = 4
LANES = 128
PANEL = 32
VMEM = pl.BlockSpec(memory_space=pltpu.VMEM)


def full_dot(a, b, ca, cb):
    return lax.dot_general(
        a,
        b,
        (((ca,), (cb,)), ((), ())),
        precision=lax.Precision.HIGHEST,
        preferred_element_type=jnp.float32,
    )


def block_pairs(blocks):
    return [(i, j) for i in range(blocks) for j in range(i, blocks)]


def gather_kernel(
    sizes, total_rows, field, fib, gram, acc, half, core_in, plane_in, mine, z_in, z_sum, plane_all, all_rows,
    own_sem, a2a_send, a2a_recv, core_send, core_recv, plane_send, plane_recv, z_send, z_recv,
    zg_send, zg_recv, pg_send, pg_recv, cg_send, cg_recv,
):
    nz, nx, ny = sizes
    planes = nx * ny
    blocks = ny
    pairs = block_pairs(blocks)
    cells = fib.shape[3]
    steps = fib.shape[1]
    half_rows = half.shape[0]
    piece = plane_in.shape[1]
    tiles = piece // 8
    z = lax.axis_index("gx")
    gy = lax.axis_index("gy")
    x = gy // 2
    c = gy % 2
    y = lax.axis_index("gz")
    p = x * ny + y

    def peer_plane(k):
        q = lax.rem(p + k, planes)
        return q, {"gy": (q // ny) * 2 + c, "gz": lax.rem(q, ny)}

    other = {"gy": x * 2 + (1 - c)}

    barrier = pltpu.get_barrier_semaphore()
    pl.semaphore_signal(barrier, inc=1, device_id=other)

    def greet_plane(k, _):
        pl.semaphore_signal(barrier, inc=1, device_id=peer_plane(k)[1])
        return 0

    def greet_z(k, _):
        pl.semaphore_signal(barrier, inc=1, device_id={"gx": lax.rem(z + k, nz)})
        return 0

    lax.fori_loop(1, planes, greet_plane, 0)
    lax.fori_loop(1, nz, greet_z, 0)
    pl.semaphore_wait(barrier, planes + nz - 1)

    sends = []
    for s in range(steps):
        for k in range(1, ny):
            to = lax.rem(y + k, ny)
            copy = pltpu.make_async_remote_copy(
                src_ref=field.at[s, :, pl.ds(to * cells, cells), :],
                dst_ref=fib.at[y, s],
                send_sem=a2a_send.at[s, k - 1],
                recv_sem=a2a_recv.at[s, k - 1],
                device_id={"gz": to},
            )
            copy.start()
            sends.append(copy)
    owns = []
    for s in range(steps):
        copy = pltpu.make_async_copy(field.at[s, :, pl.ds(y * cells, cells), :], fib.at[y, s], own_sem.at[s])
        copy.start()
        owns.append(copy)
    for s in range(steps):
        owns[s].wait()
        for k in range(1, ny):
            sends[s * (ny - 1) + k - 1].wait_recv()
        rows = jnp.concatenate([fib[b, s].reshape(-1, LANES) for b in range(blocks)], axis=1)
        for i in range(0, blocks, 2):
            term = full_dot(rows[:, i * LANES : (i + 2) * LANES], rows[:, i * LANES :], 0, 0)
            for a in (0, 1):
                for b in range(i + a, blocks):
                    n = pairs.index((i + a, b)) * LANES
                    part = term[a * LANES : (a + 1) * LANES, (b - i) * LANES : (b - i + 1) * LANES]
                    if s == 0:
                        acc[n : n + LANES, :] = part
                    else:
                        acc[n : n + LANES, :] = acc[n : n + LANES, :] + part

    keep = pl.multiple_of(c * half_rows, 8)
    give = pl.multiple_of((1 - c) * half_rows, 8)
    copy = pltpu.make_async_remote_copy(
        src_ref=acc.at[pl.ds(give, half_rows)],
        dst_ref=core_in,
        send_sem=core_send,
        recv_sem=core_recv,
        device_id=other,
    )
    copy.start()
    copy.wait_recv()
    half[...] = acc[pl.ds(keep, half_rows), :] + core_in[...]
    copy.wait_send()

    def plane_copy(k):
        q, device = peer_plane(k)
        return pltpu.make_async_remote_copy(
            src_ref=half.at[pl.ds(pl.multiple_of(q * piece, 8), piece)],
            dst_ref=plane_in.at[k - 1],
            send_sem=plane_send.at[k - 1],
            recv_sem=plane_recv.at[k - 1],
            device_id=device,
        )

    def start(make):
        def body(k, _):
            make(k).start()
            return 0

        return body

    def finish(make):
        def body(k, _):
            make(k).wait_send()
            return 0

        return body

    lax.fori_loop(1, planes, start(plane_copy), 0)

    def plane_add(k, total):
        plane_copy(k).wait_recv()
        return total + plane_in[k - 1]

    mine[...] = lax.fori_loop(1, planes, plane_add, half[pl.ds(pl.multiple_of(p * piece, 8), piece), :])

    spread = nz // tiles
    tile = lax.rem(z // spread, tiles)
    owner = (lax.rem(z, spread) == 0) & (z // spread < tiles)

    def z_copy(t):
        return pltpu.make_async_remote_copy(
            src_ref=mine.at[pl.ds(t * 8, 8)],
            dst_ref=z_in.at[z],
            send_sem=z_send.at[t],
            recv_sem=z_recv.at[z],
            device_id={"gx": t * spread},
        )

    for t in range(tiles):

        @pl.when(z != t * spread)
        def _():
            z_copy(t).start()

    @pl.when(owner)
    def _():
        def z_add(k, total):
            w = lax.rem(z + k, nz)
            pltpu.make_async_remote_copy(
                src_ref=z_in.at[w],
                dst_ref=z_in.at[w],
                send_sem=z_send.at[0],
                recv_sem=z_recv.at[w],
                device_id={"gx": w},
            ).wait_recv()
            return total + z_in[w]

        own = mine[pl.ds(pl.multiple_of(tile * 8, 8), 8), :]
        z_sum[tile] = lax.fori_loop(1, nz, z_add, own) * jnp.float32(1.0 / total_rows)

    def zg_copy(k):
        return pltpu.make_async_remote_copy(
            src_ref=z_sum.at[tile],
            dst_ref=z_sum.at[tile],
            send_sem=zg_send.at[k - 1],
            recv_sem=zg_recv.at[tile],
            device_id={"gx": lax.rem(z + k, nz)},
        )

    @pl.when(owner)
    def _():
        lax.fori_loop(1, nz, start(zg_copy), 0)

    for t in range(tiles):

        @pl.when(z != t * spread)
        def _():
            pltpu.make_async_remote_copy(
                src_ref=z_sum.at[t],
                dst_ref=z_sum.at[t],
                send_sem=zg_send.at[0],
                recv_sem=zg_recv.at[t],
                device_id={"gx": lax.rem(z + 1, nz)},
            ).wait_recv()

    plane_all[p] = z_sum[...].reshape(piece, LANES)

    def pg_copy(k):
        return pltpu.make_async_remote_copy(
            src_ref=plane_all.at[p],
            dst_ref=plane_all.at[p],
            send_sem=pg_send.at[k - 1],
            recv_sem=pg_recv.at[k - 1],
            device_id=peer_plane(k)[1],
        )

    def cg_copy(k):
        q = lax.rem(p + planes - k, planes)
        return pltpu.make_async_remote_copy(
            src_ref=plane_all.at[q],
            dst_ref=all_rows.at[q],
            send_sem=cg_send.at[k],
            recv_sem=cg_recv.at[k],
            device_id=other,
        )

    lax.fori_loop(1, planes, start(pg_copy), 0)
    cg_copy(0).start()

    def forward(k, _):
        pg_copy(k).wait_recv()
        cg_copy(k).start()
        return 0

    lax.fori_loop(1, planes, forward, 0)

    def arrived(k, _):
        cg_copy(k).wait_recv()
        return 0

    lax.fori_loop(0, planes, arrived, 0)

    def put(n, block):
        i, j = pairs[n]
        gram[i * LANES : (i + 1) * LANES, j * LANES : (j + 1) * LANES] = block
        if i != j:
            gram[j * LANES : (j + 1) * LANES, i * LANES : (i + 1) * LANES] = block.T

    here = plane_all[...].reshape(half_rows, LANES)
    there = all_rows[...].reshape(half_rows, LANES)
    low = jnp.where(c == 0, here, there)
    high = jnp.where(c == 0, there, here)
    both = jnp.concatenate([low, high], axis=0)
    for n in range(len(pairs)):
        put(n, both[n * LANES : (n + 1) * LANES, :])

    for copy in sends:
        copy.wait_send()
    lax.fori_loop(1, planes, finish(plane_copy), 0)
    for t in range(tiles):

        @pl.when(z != t * spread)
        def _():
            z_copy(t).wait_send()

    @pl.when(owner)
    def _():
        lax.fori_loop(1, nz, finish(zg_copy), 0)

    lax.fori_loop(1, planes, finish(pg_copy), 0)
    lax.fori_loop(0, planes, finish(cg_copy), 0)


def reciprocal(d):
    r = pl.reciprocal(d, approx=True)
    return r * (2.0 - d * r)


def eliminate(w, factor_t):
    wide = w.shape[1]
    rank = w.shape[0]
    groups = PANEL // 8
    rows = lax.broadcasted_iota(jnp.int32, (8, LANES), 0)

    def spread(v):
        return jnp.concatenate([v] * (wide // LANES), axis=1)

    def row(v, i):
        return jnp.broadcast_to(v[i : i + 1, :], (8, v.shape[1]))

    for j0 in range(0, rank, PANEL):
        panel = [w[j0 + 8 * g : j0 + 8 * g + 8, :] for g in range(groups)]
        cols = {}
        for k in range(PANEL):
            for g in range(k // 8, groups):
                cols[k, g] = jnp.broadcast_to(panel[g][:, j0 + k : j0 + k + 1], (8, LANES))
        scale = [jnp.ones((8, LANES), jnp.float32) for _ in range(groups)]
        for j in range(PANEL):
            gj, ij = j // 8, j % 8
            pivot = row(cols[j, gj], ij)
            inverse = reciprocal(pivot)
            if j + 1 < PANEL:
                k = j + 1
                across = row(cols[j, k // 8], k % 8)
                for g in range(k // 8, groups):
                    cols[k, g] = cols[k, g] - (cols[j, g] * across) * inverse
            multiplier = {g: cols[j, g] * inverse for g in range(gj, groups)}
            for k in range(j + 2, PANEL):
                across = row(cols[j, k // 8], k % 8)
                for g in range(k // 8, groups):
                    cols[k, g] = cols[k, g] - multiplier[g] * across
            pivot_row = row(panel[gj], ij)
            scale[gj] = jnp.where(rows == ij, lax.rsqrt(pivot), scale[gj])
            for g in range(gj, groups):
                if g > gj:
                    panel[g] = panel[g] - spread(multiplier[g]) * pivot_row
                elif ij < 7:
                    panel[g] = panel[g] - spread(jnp.where(rows > ij, multiplier[g], 0.0)) * pivot_row
        panel = [panel[g] * spread(scale[g]) for g in range(groups)]
        for g in range(groups):
            factor_t[j0 + 8 * g : j0 + 8 * g + 8, :] = panel[g][:, rank:]
        j1 = j0 + PANEL
        if j1 < rank:
            upper = jnp.concatenate(panel, axis=0)
            w[j1:, :] = w[j1:, :] - full_dot(upper[:, j1:rank], upper, 0, 0)


def factor_kernel(fib, gram, core, factor, w, factor_t):
    rank = w.shape[0]
    for step in range(ITERS):
        if step == 0:
            grown_t = gram[:rank, :]
        else:
            grown_t = full_dot(factor_t[...], gram[...], 1, 0)
        w[:, rank:] = grown_t
        w[:, :rank] = full_dot(grown_t, grown_t, 1, 1)
        eliminate(w, factor_t)
    result = factor_t[...].T
    factor[...] = result
    rows = jnp.concatenate([fib[b].reshape(-1, LANES) for b in range(fib.shape[0])], axis=1)
    core[...] = full_dot(rows, result, 1, 0)


def on_device(sizes, field):
    nz, nx, ny = sizes
    steps, width_x, width_y, width_z = field.shape
    cells = width_y // ny
    width = width_z * ny
    planes = nx * ny
    rows = steps * width_x * cells
    pair_rows = len(block_pairs(ny)) * LANES
    half = pair_rows // 2
    piece = half // planes
    tiles = piece // 8
    f32 = jnp.float32
    dma = pltpu.SemaphoreType.DMA
    fib, gram = pl.pallas_call(
        functools.partial(gather_kernel, sizes, rows * nz * nx * 2 * ny),
        out_shape=(
            jax.ShapeDtypeStruct((ny, steps, width_x, cells, width_z), f32),
            jax.ShapeDtypeStruct((width, width), f32),
        ),
        in_specs=[pl.BlockSpec(memory_space=pl.ANY)],
        out_specs=(VMEM, VMEM),
        scratch_shapes=[
            pltpu.VMEM((pair_rows, LANES), f32),
            pltpu.VMEM((half, LANES), f32),
            pltpu.VMEM((half, LANES), f32),
            pltpu.VMEM((planes - 1, piece, LANES), f32),
            pltpu.VMEM((piece, LANES), f32),
            pltpu.VMEM((nz, 8, LANES), f32),
            pltpu.VMEM((tiles, 8, LANES), f32),
            pltpu.VMEM((planes, piece, LANES), f32),
            pltpu.VMEM((planes, piece, LANES), f32),
            dma((steps,)),
            dma((steps, ny - 1)),
            dma((steps, ny - 1)),
            dma,
            dma,
            dma((planes - 1,)),
            dma((planes - 1,)),
            dma((tiles,)),
            dma((nz,)),
            dma((nz - 1,)),
            dma((tiles,)),
            dma((planes - 1,)),
            dma((planes - 1,)),
            dma((planes,)),
            dma((planes,)),
        ],
        compiler_params=pltpu.CompilerParams(
            collective_id=0, has_side_effects=True, vmem_limit_bytes=24 * 2**20
        ),
        name="gather_gram",
    )(field)
    core, factor = pl.pallas_call(
        factor_kernel,
        out_shape=(
            jax.ShapeDtypeStruct((rows, RANK), f32),
            jax.ShapeDtypeStruct((width, RANK), f32),
        ),
        in_specs=[VMEM, VMEM],
        out_specs=(VMEM, VMEM),
        scratch_shapes=[
            pltpu.VMEM((RANK, RANK + width), f32),
            pltpu.VMEM((RANK, width), f32),
        ],
        compiler_params=pltpu.CompilerParams(vmem_limit_bytes=24 * 2**20),
        name="factor_core",
    )(fib, gram)
    return core.reshape(steps, width_x, cells, RANK), factor


def solution(mesh):
    sizes = (mesh.shape["gx"], mesh.shape["gy"] // 2, mesh.shape["gz"])
    return jax.shard_map(
        functools.partial(on_device, sizes),
        mesh=mesh,
        in_specs=(P(None, "gx", "gy", "gz"),),
        out_specs=(P(None, "gx", ("gy", "gz"), None), P()),
        check_vma=False,
    )
```

```python
import functools

import jax
import jax.numpy as jnp
from jax import lax
from jax.experimental import pallas as pl
from jax.experimental.pallas import tpu as pltpu
from jax.sharding import PartitionSpec as P

RANK = 128
ITERS = 4
LANES = 128
PANEL = 32
VMEM = pl.BlockSpec(memory_space=pltpu.VMEM)


def full_dot(a, b, ca, cb):
    return lax.dot_general(
        a,
        b,
        (((ca,), (cb,)), ((), ())),
        precision=lax.Precision.HIGHEST,
        preferred_element_type=jnp.float32,
    )


def block_pairs(blocks):
    return [(i, j) for i in range(blocks) for j in range(i, blocks)]


def ring(n, k):
    return min(k % n, -k % n)


def gather_kernel(
    sizes, total_rows, field, fib, sums, acc, half, core_in, plane_in, mine, z_in, z_sum,
    known, own_sem, a2a_send, a2a_recv, core_send, core_recv, plane_send, plane_recv, z_send, z_recv,
    zg_send, zg_recv, pg_send, pg_recv, cg_send, cg_recv,
):
    nz, nx, ny = sizes
    planes = nx * ny
    blocks = ny
    pairs = block_pairs(blocks)
    cells = fib.shape[3]
    steps = fib.shape[1]
    half_rows = half.shape[0]
    piece = plane_in.shape[1]
    tiles = piece // 8
    z = lax.axis_index("gx")
    gy = lax.axis_index("gy")
    x = gy // 2
    c = gy % 2
    y = lax.axis_index("gz")
    p = x * ny + y

    def at_x(k):
        return {"gy": lax.rem(x + k % nx, nx) * 2 + c}

    def at_y(k):
        return {"gz": lax.rem(y + k % ny, ny)}

    def at_z(k):
        return {"gx": lax.rem(z + k % nz, nz)}

    other = {"gy": x * 2 + (1 - c)}

    barrier = pltpu.get_barrier_semaphore()
    near = [at_y(k) for k in range(1, ny)] + [other, at_x(1), at_x(-1), at_z(1), at_z(-1)]
    for device in near:
        pl.semaphore_signal(barrier, inc=1, device_id=device)
    pl.semaphore_wait(barrier, len(near))

    sends = []
    order = sorted(range(1, ny), key=lambda k: -ring(ny, k))
    for s in range(steps):
        for k in order:
            to = lax.rem(y + k, ny)
            copy = pltpu.make_async_remote_copy(
                src_ref=field.at[s, :, pl.ds(to * cells, cells), :],
                dst_ref=fib.at[y, s],
                send_sem=a2a_send.at[s, k - 1],
                recv_sem=a2a_recv.at[s, k - 1],
                device_id={"gz": to},
            )
            copy.start()
            sends.append(copy)
    owns = []
    for s in range(steps):
        copy = pltpu.make_async_copy(field.at[s, :, pl.ds(y * cells, cells), :], fib.at[y, s], own_sem.at[s])
        copy.start()
        owns.append(copy)

    rounds = [[at_x(1), at_x(-1), at_z(1), at_z(-1)], [at_z(2), at_z(-2)], [at_z(4), at_z(-4)]]
    if nx > 2:
        rounds[1].append(at_x(2))
    for i, devices in enumerate(rounds):
        for device in devices:
            pl.semaphore_signal(known.at[i], inc=1, device_id=device)
        pl.semaphore_wait(known.at[i], len(devices))

    for s in range(steps):
        owns[s].wait()
        for i in range(ny - 1):
            sends[s * (ny - 1) + i].wait_recv()
        rows = jnp.concatenate([fib[b, s].reshape(-1, LANES) for b in range(blocks)], axis=1)
        for i in range(0, blocks, 2):
            term = full_dot(rows[:, i * LANES : (i + 2) * LANES], rows[:, i * LANES :], 0, 0)
            for a in (0, 1):
                for b in range(i + a, blocks):
                    n = pairs.index((i + a, b)) * LANES
                    part = term[a * LANES : (a + 1) * LANES, (b - i) * LANES : (b - i + 1) * LANES]
                    if s == 0:
                        acc[n : n + LANES, :] = part
                    else:
                        acc[n : n + LANES, :] = acc[n : n + LANES, :] + part

    keep = pl.multiple_of(c * half_rows, 8)
    give = pl.multiple_of((1 - c) * half_rows, 8)
    core_copy = pltpu.make_async_remote_copy(
        src_ref=acc.at[pl.ds(give, half_rows)],
        dst_ref=core_in,
        send_sem=core_send,
        recv_sem=core_recv,
        device_id=other,
    )
    core_copy.start()
    core_copy.wait_recv()
    half[...] = acc[pl.ds(keep, half_rows), :] + core_in[...]

    offsets = [(i, j) for i in range(nx) for j in range(ny) if (i, j) != (0, 0)]
    offsets.sort(key=lambda o: -(ring(nx, o[0]) + ring(ny, o[1])))

    def plane_at(i, j):
        to_x, to_y = lax.rem(x + i % nx, nx), lax.rem(y + j % ny, ny)
        return to_x * ny + to_y, {"gy": to_x * 2 + c, "gz": to_y}

    plane_copies = []
    for n, (i, j) in enumerate(offsets):
        q, device = plane_at(i, j)
        copy = pltpu.make_async_remote_copy(
            src_ref=half.at[pl.ds(pl.multiple_of(q * piece, 8), piece)],
            dst_ref=plane_in.at[n],
            send_sem=plane_send.at[n],
            recv_sem=plane_recv.at[n],
            device_id=device,
        )
        copy.start()
        plane_copies.append(copy)
    total = half[pl.ds(pl.multiple_of(p * piece, 8), piece), :]
    for n in reversed(range(len(offsets))):
        plane_copies[n].wait_recv()
        total = total + plane_in[n]
    mine[...] = total

    spread = nz // tiles
    tile = lax.rem(z // spread, tiles)
    owner = (lax.rem(z, spread) == 0) & (z // spread < tiles)
    distances = sorted(range(1, nz), key=lambda k: -ring(nz, k))

    def z_copy(t):
        return pltpu.make_async_remote_copy(
            src_ref=mine.at[pl.ds(t * 8, 8)],
            dst_ref=z_in.at[z],
            send_sem=z_send.at[t],
            recv_sem=z_recv.at[z],
            device_id={"gx": t * spread},
        )

    def zg_copy(i, t):
        return pltpu.make_async_remote_copy(
            src_ref=z_sum.at[t],
            dst_ref=z_sum.at[t],
            send_sem=zg_send.at[i],
            recv_sem=zg_recv.at[t],
            device_id=at_z(distances[i]),
        )

    for t in range(tiles):

        @pl.when(z != t * spread)
        def _():
            z_copy(t).start()

    @pl.when(owner)
    def _():
        total = mine[pl.ds(pl.multiple_of(tile * 8, 8), 8), :]
        for k in reversed(distances):
            w = lax.rem(z + k, nz)
            pltpu.make_async_remote_copy(
                src_ref=z_in.at[w],
                dst_ref=z_in.at[w],
                send_sem=z_send.at[0],
                recv_sem=z_recv.at[w],
                device_id={"gx": w},
            ).wait_recv()
            total = total + z_in[w]
        z_sum[tile] = total * jnp.float32(1.0 / total_rows)
        for i in range(nz - 1):
            zg_copy(i, tile).start()

    for t in range(tiles):

        @pl.when(z != t * spread)
        def _():
            zg_copy(0, t).wait_recv()

    sums[c, p] = z_sum[...].reshape(piece, LANES)

    def cg_copy(n, q):
        return pltpu.make_async_remote_copy(
            src_ref=sums.at[c, q],
            dst_ref=sums.at[c, q],
            send_sem=cg_send.at[n],
            recv_sem=cg_recv.at[n],
            device_id=other,
        )

    pg_copies, cg_copies = [], []
    for n, (i, j) in enumerate(offsets):
        copy = pltpu.make_async_remote_copy(
            src_ref=sums.at[c, p],
            dst_ref=sums.at[c, p],
            send_sem=pg_send.at[n],
            recv_sem=pg_recv.at[n],
            device_id=plane_at(i, j)[1],
        )
        copy.start()
        pg_copies.append(copy)
    cg_copies.append(cg_copy(len(offsets), p))
    cg_copies[-1].start()
    for n in reversed(range(len(offsets))):
        i, j = offsets[n]
        pg_copies[n].wait_recv()
        cg_copies.append(cg_copy(n, plane_at(-i, -j)[0]))
        cg_copies[-1].start()

    for copy in sends + [core_copy] + plane_copies + pg_copies:
        copy.wait_send()
    for t in range(tiles):

        @pl.when(z != t * spread)
        def _():
            z_copy(t).wait_send()

    @pl.when(owner)
    def _():
        for i in range(nz - 1):
            zg_copy(i, tile).wait_send()

    for copy in cg_copies:
        copy.wait()


def reciprocal(d):
    r = pl.reciprocal(d, approx=True)
    return r * (2.0 - d * r)


def eliminate(w, factor_t):
    wide = w.shape[1]
    rank = w.shape[0]
    groups = PANEL // 8
    rows = lax.broadcasted_iota(jnp.int32, (8, LANES), 0)

    def spread(v):
        return jnp.concatenate([v] * (wide // LANES), axis=1)

    def row(v, i):
        return jnp.broadcast_to(v[i : i + 1, :], (8, v.shape[1]))

    for j0 in range(0, rank, PANEL):
        panel = [w[j0 + 8 * g : j0 + 8 * g + 8, :] for g in range(groups)]
        cols = {}
        for k in range(PANEL):
            for g in range(k // 8, groups):
                cols[k, g] = jnp.broadcast_to(panel[g][:, j0 + k : j0 + k + 1], (8, LANES))
        scale = [jnp.ones((8, LANES), jnp.float32) for _ in range(groups)]
        for j in range(PANEL):
            gj, ij = j // 8, j % 8
            pivot = row(cols[j, gj], ij)
            inverse = reciprocal(pivot)
            if j + 1 < PANEL:
                k = j + 1
                across = row(cols[j, k // 8], k % 8)
                for g in range(k // 8, groups):
                    cols[k, g] = cols[k, g] - (cols[j, g] * across) * inverse
            multiplier = {g: cols[j, g] * inverse for g in range(gj, groups)}
            for k in range(j + 2, PANEL):
                across = row(cols[j, k // 8], k % 8)
                for g in range(k // 8, groups):
                    cols[k, g] = cols[k, g] - multiplier[g] * across
            pivot_row = row(panel[gj], ij)
            scale[gj] = jnp.where(rows == ij, lax.rsqrt(pivot), scale[gj])
            for g in range(gj, groups):
                if g > gj:
                    panel[g] = panel[g] - spread(multiplier[g]) * pivot_row
                elif ij < 7:
                    panel[g] = panel[g] - spread(jnp.where(rows > ij, multiplier[g], 0.0)) * pivot_row
        panel = [panel[g] * spread(scale[g]) for g in range(groups)]
        for g in range(groups):
            factor_t[j0 + 8 * g : j0 + 8 * g + 8, :] = panel[g][:, rank:]
        j1 = j0 + PANEL
        if j1 < rank:
            upper = jnp.concatenate(panel, axis=0)
            w[j1:, :] = w[j1:, :] - full_dot(upper[:, j1:rank], upper, 0, 0)


def factor_kernel(fib, sums, core, factor, gram, w, factor_t):
    rank = w.shape[0]
    blocks = fib.shape[0]
    pairs = block_pairs(blocks)
    part = [sums[n * LANES : (n + 1) * LANES, :] for n in range(len(pairs))]
    for step in range(ITERS):
        if step == 0:
            grown_t = jnp.concatenate(part[:blocks], axis=1)
        else:
            grown_t = full_dot(factor_t[...], gram[...], 1, 0)
        w[:, rank:] = grown_t
        w[:, :rank] = full_dot(grown_t, grown_t, 1, 1)
        eliminate(w, factor_t)
        if step == 0:
            for n, (i, j) in enumerate(pairs):
                gram[i * LANES : (i + 1) * LANES, j * LANES : (j + 1) * LANES] = part[n]
                if i != j:
                    gram[j * LANES : (j + 1) * LANES, i * LANES : (i + 1) * LANES] = part[n].T
    result = factor_t[...].T
    factor[...] = result
    rows = jnp.concatenate([fib[b].reshape(-1, LANES) for b in range(blocks)], axis=1)
    core[...] = full_dot(rows, result, 1, 0)


def on_device(sizes, field):
    nz, nx, ny = sizes
    steps, width_x, width_y, width_z = field.shape
    cells = width_y // ny
    width = width_z * ny
    planes = nx * ny
    rows = steps * width_x * cells
    pair_rows = len(block_pairs(ny)) * LANES
    half = pair_rows // 2
    piece = half // planes
    tiles = piece // 8
    f32 = jnp.float32
    dma = pltpu.SemaphoreType.DMA
    fib, sums = pl.pallas_call(
        functools.partial(gather_kernel, sizes, rows * nz * nx * 2 * ny),
        out_shape=(
            jax.ShapeDtypeStruct((ny, steps, width_x, cells, width_z), f32),
            jax.ShapeDtypeStruct((2, planes, piece, LANES), f32),
        ),
        in_specs=[pl.BlockSpec(memory_space=pl.ANY)],
        out_specs=(VMEM, VMEM),
        scratch_shapes=[
            pltpu.VMEM((pair_rows, LANES), f32),
            pltpu.VMEM((half, LANES), f32),
            pltpu.VMEM((half, LANES), f32),
            pltpu.VMEM((planes - 1, piece, LANES), f32),
            pltpu.VMEM((piece, LANES), f32),
            pltpu.VMEM((nz, 8, LANES), f32),
            pltpu.VMEM((tiles, 8, LANES), f32),
            pltpu.SemaphoreType.REGULAR((3,)),
            dma((steps,)),
            dma((steps, ny - 1)),
            dma((steps, ny - 1)),
            dma,
            dma,
            dma((planes - 1,)),
            dma((planes - 1,)),
            dma((tiles,)),
            dma((nz,)),
            dma((nz - 1,)),
            dma((tiles,)),
            dma((planes - 1,)),
            dma((planes - 1,)),
            dma((planes,)),
            dma((planes,)),
        ],
        compiler_params=pltpu.CompilerParams(
            collective_id=0, has_side_effects=True, vmem_limit_bytes=24 * 2**20
        ),
        name="gather_gram",
    )(field)
    core, factor = pl.pallas_call(
        factor_kernel,
        out_shape=(
            jax.ShapeDtypeStruct((rows, RANK), f32),
            jax.ShapeDtypeStruct((width, RANK), f32),
        ),
        in_specs=[VMEM, VMEM],
        out_specs=(VMEM, VMEM),
        scratch_shapes=[
            pltpu.VMEM((width, width), f32),
            pltpu.VMEM((RANK, RANK + width), f32),
            pltpu.VMEM((RANK, width), f32),
        ],
        compiler_params=pltpu.CompilerParams(vmem_limit_bytes=24 * 2**20),
        name="factor_core",
    )(fib, sums.reshape(pair_rows, LANES))
    return core.reshape(steps, width_x, cells, RANK), factor


def solution(mesh):
    sizes = (mesh.shape["gx"], mesh.shape["gy"] // 2, mesh.shape["gz"])
    return jax.shard_map(
        functools.partial(on_device, sizes),
        mesh=mesh,
        in_specs=(P(None, "gx", "gy", "gz"),),
        out_specs=(P(None, "gx", ("gy", "gz"), None), P()),
        check_vma=False,
    )
```

```python
import functools

import jax
import jax.numpy as jnp
from jax import lax
from jax.experimental import pallas as pl
from jax.experimental.pallas import tpu as pltpu
from jax.sharding import PartitionSpec as P

RANK = 128
ITERS = 4
LANES = 128
PANEL = 32
BLOCK = 16
VMEM = pl.BlockSpec(memory_space=pltpu.VMEM)


def full_dot(a, b, ca, cb):
    return lax.dot_general(
        a,
        b,
        (((ca,), (cb,)), ((), ())),
        precision=lax.Precision.HIGHEST,
        preferred_element_type=jnp.float32,
    )


def block_pairs(blocks):
    return [(i, j) for i in range(blocks) for j in range(i, blocks)]


def ring(n, k):
    return min(k % n, -k % n)


def gather_kernel(
    sizes, total_rows, field, fib, sums, acc, half, core_in, plane_in, mine, z_in, z_sum,
    known, own_sem, a2a_send, a2a_recv, core_send, core_recv, plane_send, plane_recv, z_send, z_recv,
    zg_send, zg_recv, pg_send, pg_recv, cg_send, cg_recv,
):
    nz, nx, ny = sizes
    planes = nx * ny
    blocks = ny
    pairs = block_pairs(blocks)
    cells = fib.shape[3]
    steps = fib.shape[1]
    half_rows = half.shape[0]
    piece = plane_in.shape[1]
    tiles = piece // 8
    z = lax.axis_index("gx")
    gy = lax.axis_index("gy")
    x = gy // 2
    c = gy % 2
    y = lax.axis_index("gz")
    p = x * ny + y

    def at_x(k):
        return {"gy": lax.rem(x + k % nx, nx) * 2 + c}

    def at_y(k):
        return {"gz": lax.rem(y + k % ny, ny)}

    def at_z(k):
        return {"gx": lax.rem(z + k % nz, nz)}

    other = {"gy": x * 2 + (1 - c)}

    barrier = pltpu.get_barrier_semaphore()
    near = [at_y(k) for k in range(1, ny)] + [other, at_x(1), at_x(-1), at_z(1), at_z(-1)]
    for device in near:
        pl.semaphore_signal(barrier, inc=1, device_id=device)
    pl.semaphore_wait(barrier, len(near))

    sends = []
    order = sorted(range(1, ny), key=lambda k: -ring(ny, k))
    for s in range(steps):
        for k in order:
            to = lax.rem(y + k, ny)
            copy = pltpu.make_async_remote_copy(
                src_ref=field.at[s, :, pl.ds(to * cells, cells), :],
                dst_ref=fib.at[y, s],
                send_sem=a2a_send.at[s, k - 1],
                recv_sem=a2a_recv.at[s, k - 1],
                device_id={"gz": to},
            )
            copy.start()
            sends.append(copy)
    owns = []
    for s in range(steps):
        copy = pltpu.make_async_copy(field.at[s, :, pl.ds(y * cells, cells), :], fib.at[y, s], own_sem.at[s])
        copy.start()
        owns.append(copy)

    rounds = [[at_x(1), at_x(-1), at_z(1), at_z(-1)], [at_z(2), at_z(-2)], [at_z(4), at_z(-4)]]
    if nx > 2:
        rounds[1].append(at_x(2))
    for i, devices in enumerate(rounds):
        for device in devices:
            pl.semaphore_signal(known.at[i], inc=1, device_id=device)
        pl.semaphore_wait(known.at[i], len(devices))

    for s in range(steps):
        owns[s].wait()
        for i in range(ny - 1):
            sends[s * (ny - 1) + i].wait_recv()
        rows = jnp.concatenate([fib[b, s].reshape(-1, LANES) for b in range(blocks)], axis=1)
        for i in range(0, blocks, 2):
            term = full_dot(rows[:, i * LANES : (i + 2) * LANES], rows[:, i * LANES :], 0, 0)
            for a in (0, 1):
                for b in range(i + a, blocks):
                    n = pairs.index((i + a, b)) * LANES
                    part = term[a * LANES : (a + 1) * LANES, (b - i) * LANES : (b - i + 1) * LANES]
                    if s == 0:
                        acc[n : n + LANES, :] = part
                    else:
                        acc[n : n + LANES, :] = acc[n : n + LANES, :] + part

    keep = pl.multiple_of(c * half_rows, 8)
    give = pl.multiple_of((1 - c) * half_rows, 8)
    core_copy = pltpu.make_async_remote_copy(
        src_ref=acc.at[pl.ds(give, half_rows)],
        dst_ref=core_in,
        send_sem=core_send,
        recv_sem=core_recv,
        device_id=other,
    )
    core_copy.start()
    core_copy.wait_recv()
    half[...] = acc[pl.ds(keep, half_rows), :] + core_in[...]

    offsets = [(i, j) for i in range(nx) for j in range(ny) if (i, j) != (0, 0)]
    offsets.sort(key=lambda o: -(ring(nx, o[0]) + ring(ny, o[1])))

    def plane_at(i, j):
        to_x, to_y = lax.rem(x + i % nx, nx), lax.rem(y + j % ny, ny)
        return to_x * ny + to_y, {"gy": to_x * 2 + c, "gz": to_y}

    plane_copies = []
    for n, (i, j) in enumerate(offsets):
        q, device = plane_at(i, j)
        copy = pltpu.make_async_remote_copy(
            src_ref=half.at[pl.ds(pl.multiple_of(q * piece, 8), piece)],
            dst_ref=plane_in.at[n],
            send_sem=plane_send.at[n],
            recv_sem=plane_recv.at[n],
            device_id=device,
        )
        copy.start()
        plane_copies.append(copy)
    total = half[pl.ds(pl.multiple_of(p * piece, 8), piece), :]
    for n in reversed(range(len(offsets))):
        plane_copies[n].wait_recv()
        total = total + plane_in[n]
    mine[...] = total

    spread = nz // tiles
    tile = lax.rem(z // spread, tiles)
    owner = (lax.rem(z, spread) == 0) & (z // spread < tiles)
    distances = sorted(range(1, nz), key=lambda k: -ring(nz, k))

    def z_copy(t):
        return pltpu.make_async_remote_copy(
            src_ref=mine.at[pl.ds(t * 8, 8)],
            dst_ref=z_in.at[z],
            send_sem=z_send.at[t],
            recv_sem=z_recv.at[z],
            device_id={"gx": t * spread},
        )

    def zg_copy(i, t):
        return pltpu.make_async_remote_copy(
            src_ref=z_sum.at[t],
            dst_ref=z_sum.at[t],
            send_sem=zg_send.at[i],
            recv_sem=zg_recv.at[t],
            device_id=at_z(distances[i]),
        )

    for t in range(tiles):

        @pl.when(z != t * spread)
        def _():
            z_copy(t).start()

    @pl.when(owner)
    def _():
        total = mine[pl.ds(pl.multiple_of(tile * 8, 8), 8), :]
        for k in reversed(distances):
            w = lax.rem(z + k, nz)
            pltpu.make_async_remote_copy(
                src_ref=z_in.at[w],
                dst_ref=z_in.at[w],
                send_sem=z_send.at[0],
                recv_sem=z_recv.at[w],
                device_id={"gx": w},
            ).wait_recv()
            total = total + z_in[w]
        z_sum[tile] = total * jnp.float32(1.0 / total_rows)
        for i in range(nz - 1):
            zg_copy(i, tile).start()

    for t in range(tiles):

        @pl.when(z != t * spread)
        def _():
            zg_copy(0, t).wait_recv()

    sums[c, p] = z_sum[...].reshape(piece, LANES)

    def cg_copy(n, q):
        return pltpu.make_async_remote_copy(
            src_ref=sums.at[c, q],
            dst_ref=sums.at[c, q],
            send_sem=cg_send.at[n],
            recv_sem=cg_recv.at[n],
            device_id=other,
        )

    pg_copies, cg_copies = [], []
    for n, (i, j) in enumerate(offsets):
        copy = pltpu.make_async_remote_copy(
            src_ref=sums.at[c, p],
            dst_ref=sums.at[c, p],
            send_sem=pg_send.at[n],
            recv_sem=pg_recv.at[n],
            device_id=plane_at(i, j)[1],
        )
        copy.start()
        pg_copies.append(copy)
    cg_copies.append(cg_copy(len(offsets), p))
    cg_copies[-1].start()
    for n in reversed(range(len(offsets))):
        i, j = offsets[n]
        pg_copies[n].wait_recv()
        cg_copies.append(cg_copy(n, plane_at(-i, -j)[0]))
        cg_copies[-1].start()

    for copy in sends + [core_copy] + plane_copies + pg_copies:
        copy.wait_send()
    for t in range(tiles):

        @pl.when(z != t * spread)
        def _():
            z_copy(t).wait_send()

    @pl.when(owner)
    def _():
        for i in range(nz - 1):
            zg_copy(i, tile).wait_send()

    for copy in cg_copies:
        copy.wait()


def reciprocal(d):
    r = pl.reciprocal(d, approx=True)
    return r * (2.0 - d * r)


def short_dot(a, b, ca, cb):
    return lax.dot_general(a, b, (((ca,), (cb,)), ((), ())), preferred_element_type=jnp.float32)


def split(v):
    high = v.astype(jnp.bfloat16)
    rest = v - high.astype(jnp.float32)
    middle = rest.astype(jnp.bfloat16)
    return high, middle, (rest - middle.astype(jnp.float32)).astype(jnp.bfloat16)


def left(v, axis):
    h, m, t = split(v)
    return jnp.concatenate([h, h, m, m, h, t], axis=axis)


def right(v, axis):
    h, m, t = split(v)
    return jnp.concatenate([h, m, h, m, t, h], axis=axis)


def row(v, i):
    return jnp.broadcast_to(v[i : i + 1, :], (8, v.shape[1]))


def inverse_lower(inner):
    rank = inner.shape[0]
    count, groups = rank // PANEL, PANEL // 8
    row8 = lax.broadcasted_iota(jnp.int32, (8, rank), 0)
    lane8 = lax.broadcasted_iota(jnp.int32, (8, rank), 1)
    row_of = lax.broadcasted_iota(jnp.int32, (PANEL, rank), 0)
    lane_of = lax.broadcasted_iota(jnp.int32, (PANEL, rank), 1)
    rest = [inner[t * PANEL : (t + 1) * PANEL] for t in range(count)]
    result = []
    for s in range(count):
        j0, j1 = s * PANEL, (s + 1) * PANEL
        panel = [rest[s][8 * g : 8 * g + 8, :] for g in range(groups)]
        done = {}
        for g0 in range(0, groups, BLOCK // 8):
            c0 = j0 + 8 * g0
            cols = {}
            for k in range(BLOCK):
                for g in range(g0 + k // 8, groups):
                    cols[k, g] = jnp.broadcast_to(panel[g][:, c0 + k : c0 + k + 1], (8, rank))

            def at(j, k):
                return row(cols[j, g0 + k // 8], k % 8)

            p, q, r = at(0, 0), at(0, 1), at(1, 1)
            for j in range(0, BLOCK, 2):
                gj, ij = g0 + j // 8, j % 8
                column = c0 + j
                det = p * r - q * q
                inv = reciprocal(det)
                following = None
                if j + 2 < BLOCK:
                    k = j + 2
                    u1, u2, v1, v2 = at(j, k), at(j + 1, k), at(j, k + 1), at(j + 1, k + 1)
                    a1, a2 = r * u1 - q * u2, p * u2 - q * u1
                    e1, e2 = r * v1 - q * v2, p * v2 - q * v1
                    following = (
                        at(k, k) - (a1 * u1 + a2 * u2) * inv,
                        at(k, k + 1) - (a1 * v1 + a2 * v2) * inv,
                        at(k + 1, k + 1) - (e1 * v1 + e2 * v2) * inv,
                    )
                pi, qi, ri = p * inv, q * inv, r * inv
                first = gj + 1 if ij == 6 else gj
                m1 = {g: cols[j, g] * ri - cols[j + 1, g] * qi for g in range(first, groups)}
                m2 = {g: cols[j + 1, g] * pi - cols[j, g] * qi for g in range(first, groups)}
                for k in range(j + 2, BLOCK):
                    w1, w2 = at(j, k), at(j + 1, k)
                    for g in range(g0 + k // 8, groups):
                        cols[k, g] = cols[k, g] - (m1[g] * w1 + m2[g] * w2)
                here = lane8 // 2 == column // 2
                row1 = jnp.where(here, jnp.where(lane8 == column, 1.0, 0.0), row(panel[gj], ij))
                row2 = jnp.where(here, jnp.where(lane8 == column, 0.0, 1.0), row(panel[gj], ij + 1))
                inv_p = reciprocal(p)
                done[8 * gj + ij] = row1 * lax.rsqrt(p)
                done[8 * gj + ij + 1] = (row2 - (q * inv_p) * row1) * lax.rsqrt(det * inv_p)
                for g in range(first, groups):
                    panel[g] = jnp.where(here, 0.0, panel[g]) - (m1[g] * row1 + m2[g] * row2)
                if following:
                    p, q, r = following
        upper = []
        for g in range(groups):
            v = done[8 * g]
            for i in range(1, 8):
                v = jnp.where(row8 == i, done[8 * g + i], v)
            upper.append(v)
        upper = jnp.concatenate(upper, axis=0)
        lower = lane_of <= row_of + j0
        result.append(jnp.where(lower, upper, 0.0))
        if s + 1 < count:
            kept = jnp.where(lower | (lane_of >= j1), upper, 0.0)
            change = short_dot(left(upper, 0)[:, j1:], right(kept, 0), 0, 0)
            block = (lane_of >= j0) & (lane_of < j1)
            for t in range(s + 1, count):
                part = change[(t - s - 1) * PANEL : (t - s) * PANEL]
                rest[t] = jnp.where(block, 0.0, rest[t]) - part
    return jnp.concatenate(result, axis=0)


def factor_kernel(fib, sums, core, factor, gram):
    blocks = fib.shape[0]
    width = blocks * LANES
    pairs = block_pairs(blocks)
    part = [sums[n * LANES : (n + 1) * LANES, :] for n in range(len(pairs))]
    for n, (i, j) in enumerate(pairs):
        gram[i * LANES : (i + 1) * LANES, j * LANES : (j + 1) * LANES] = part[n]
        if i != j:
            gram[j * LANES : (j + 1) * LANES, i * LANES : (i + 1) * LANES] = part[n].T
    grown_t = jnp.concatenate(part[:blocks], axis=1)
    for step in range(ITERS):
        inner = full_dot(grown_t, grown_t, 1, 1)
        if step < ITERS - 1:
            ready = right(full_dot(grown_t, gram[...], 1, 0), 0)
            grown_t = short_dot(left(inverse_lower(inner), 1), ready, 1, 0)
        else:
            rows = jnp.concatenate([fib[b].reshape(-1, LANES) for b in range(blocks)], axis=1)
            ready = left(jnp.concatenate([grown_t.T, full_dot(rows, grown_t, 1, 1)], axis=0), 1)
            both = short_dot(ready, right(inverse_lower(inner), 1), 1, 1)
            factor[...] = both[:width]
            core[...] = both[width:]


def on_device(sizes, field):
    nz, nx, ny = sizes
    steps, width_x, width_y, width_z = field.shape
    cells = width_y // ny
    width = width_z * ny
    planes = nx * ny
    rows = steps * width_x * cells
    pair_rows = len(block_pairs(ny)) * LANES
    half = pair_rows // 2
    piece = half // planes
    tiles = piece // 8
    f32 = jnp.float32
    dma = pltpu.SemaphoreType.DMA
    fib, sums = pl.pallas_call(
        functools.partial(gather_kernel, sizes, rows * nz * nx * 2 * ny),
        out_shape=(
            jax.ShapeDtypeStruct((ny, steps, width_x, cells, width_z), f32),
            jax.ShapeDtypeStruct((2, planes, piece, LANES), f32),
        ),
        in_specs=[pl.BlockSpec(memory_space=pl.ANY)],
        out_specs=(VMEM, VMEM),
        scratch_shapes=[
            pltpu.VMEM((pair_rows, LANES), f32),
            pltpu.VMEM((half, LANES), f32),
            pltpu.VMEM((half, LANES), f32),
            pltpu.VMEM((planes - 1, piece, LANES), f32),
            pltpu.VMEM((piece, LANES), f32),
            pltpu.VMEM((nz, 8, LANES), f32),
            pltpu.VMEM((tiles, 8, LANES), f32),
            pltpu.SemaphoreType.REGULAR((3,)),
            dma((steps,)),
            dma((steps, ny - 1)),
            dma((steps, ny - 1)),
            dma,
            dma,
            dma((planes - 1,)),
            dma((planes - 1,)),
            dma((tiles,)),
            dma((nz,)),
            dma((nz - 1,)),
            dma((tiles,)),
            dma((planes - 1,)),
            dma((planes - 1,)),
            dma((planes,)),
            dma((planes,)),
        ],
        compiler_params=pltpu.CompilerParams(
            collective_id=0, has_side_effects=True, vmem_limit_bytes=24 * 2**20
        ),
        name="gather_gram",
    )(field)
    core, factor = pl.pallas_call(
        factor_kernel,
        out_shape=(
            jax.ShapeDtypeStruct((rows, RANK), f32),
            jax.ShapeDtypeStruct((width, RANK), f32),
        ),
        in_specs=[VMEM, VMEM],
        out_specs=(VMEM, VMEM),
        scratch_shapes=[
            pltpu.VMEM((width, width), f32),
        ],
        compiler_params=pltpu.CompilerParams(vmem_limit_bytes=24 * 2**20),
        name="factor_core",
    )(fib, sums.reshape(pair_rows, LANES))
    return core.reshape(steps, width_x, cells, RANK), factor


def solution(mesh):
    sizes = (mesh.shape["gx"], mesh.shape["gy"] // 2, mesh.shape["gz"])
    return jax.shard_map(
        functools.partial(on_device, sizes),
        mesh=mesh,
        in_specs=(P(None, "gx", "gy", "gz"),),
        out_specs=(P(None, "gx", ("gy", "gz"), None), P()),
        check_vma=False,
    )
```

```python
import functools

import jax
import jax.numpy as jnp
from jax import lax
from jax.experimental import pallas as pl
from jax.experimental.pallas import tpu as pltpu
from jax.sharding import PartitionSpec as P

RANK = 128
ITERS = 4
LANES = 128
PANEL = 32
BLOCK = 16
VMEM = pl.BlockSpec(memory_space=pltpu.VMEM)


def full_dot(a, b, ca, cb):
    return lax.dot_general(
        a,
        b,
        (((ca,), (cb,)), ((), ())),
        precision=lax.Precision.HIGHEST,
        preferred_element_type=jnp.float32,
    )


def block_pairs(blocks):
    return [(i, j) for i in range(blocks) for j in range(i, blocks)]


def ring(n, k):
    return min(k % n, -k % n)


def gather_kernel(
    sizes, total_rows, field, fib, sums, acc, half, core_in, plane_in, mine, z_in, z_sum,
    known, own_sem, a2a_send, a2a_recv, core_send, core_recv, plane_send, plane_recv, z_send, z_recv,
    zg_send, zg_recv, pg_send, pg_recv, cg_send, cg_recv,
):
    nz, nx, ny = sizes
    planes = nx * ny
    blocks = ny
    pairs = block_pairs(blocks)
    cells = fib.shape[3]
    steps = fib.shape[1]
    half_rows = half.shape[0]
    piece = plane_in.shape[1]
    tiles = piece // 8
    z = lax.axis_index("gx")
    gy = lax.axis_index("gy")
    x = gy // 2
    c = gy % 2
    y = lax.axis_index("gz")
    p = x * ny + y

    def at_x(k):
        return {"gy": lax.rem(x + k % nx, nx) * 2 + c}

    def at_y(k):
        return {"gz": lax.rem(y + k % ny, ny)}

    def at_z(k):
        return {"gx": lax.rem(z + k % nz, nz)}

    other = {"gy": x * 2 + (1 - c)}

    barrier = pltpu.get_barrier_semaphore()
    near = [at_y(k) for k in range(1, ny)] + [other, at_x(1), at_x(-1), at_z(1), at_z(-1)]
    for device in near:
        pl.semaphore_signal(barrier, inc=1, device_id=device)
    pl.semaphore_wait(barrier, len(near))

    deep = fib.shape[2] // 2
    chunks = [(s, pl.ds(h * deep, deep)) for s in range(steps) for h in range(2)]
    sends = []
    order = sorted(range(1, ny), key=lambda k: -ring(ny, k))
    for n, (s, part) in enumerate(chunks):
        for k in order:
            to = lax.rem(y + k, ny)
            copy = pltpu.make_async_remote_copy(
                src_ref=field.at[s, part, pl.ds(to * cells, cells), :],
                dst_ref=fib.at[y, s, part],
                send_sem=a2a_send.at[n, k - 1],
                recv_sem=a2a_recv.at[n, k - 1],
                device_id={"gz": to},
            )
            copy.start()
            sends.append(copy)
    owns = []
    for n, (s, part) in enumerate(chunks):
        copy = pltpu.make_async_copy(
            field.at[s, part, pl.ds(y * cells, cells), :], fib.at[y, s, part], own_sem.at[n]
        )
        copy.start()
        owns.append(copy)

    rounds = [[at_x(1), at_x(-1), at_z(1), at_z(-1)], [at_z(2), at_z(-2)], [at_z(4), at_z(-4)]]
    if nx > 2:
        rounds[1].append(at_x(2))
    for i, devices in enumerate(rounds):
        for device in devices:
            pl.semaphore_signal(known.at[i], inc=1, device_id=device)
        pl.semaphore_wait(known.at[i], len(devices))

    for n, (s, _) in enumerate(chunks):
        owns[n].wait()
        for i in range(ny - 1):
            sends[n * (ny - 1) + i].wait_recv()
        x0 = (n % 2) * deep
        rows = jnp.concatenate([fib[b, s, x0 : x0 + deep].reshape(-1, LANES) for b in range(blocks)], axis=1)
        for i in range(0, blocks, 2):
            term = full_dot(rows[:, i * LANES : (i + 2) * LANES], rows[:, i * LANES :], 0, 0)
            for a in (0, 1):
                for b in range(i + a, blocks):
                    r = pairs.index((i + a, b)) * LANES
                    part = term[a * LANES : (a + 1) * LANES, (b - i) * LANES : (b - i + 1) * LANES]
                    if n == 0:
                        acc[r : r + LANES, :] = part
                    else:
                        acc[r : r + LANES, :] = acc[r : r + LANES, :] + part

    offsets = [(i, j) for i in range(nx) for j in range(ny) if (i, j) != (0, 0)]
    offsets.sort(key=lambda o: -(ring(nx, o[0]) + ring(ny, o[1])))

    def plane_at(i, j):
        to_x, to_y = lax.rem(x + i % nx, nx), lax.rem(y + j % ny, ny)
        return to_x * ny + to_y, {"gy": to_x * 2 + c, "gz": to_y}

    def rows_of(start, q):
        return pl.ds(pl.multiple_of(start + q * piece, 8), piece)

    keep = c * half_rows
    give = (1 - c) * half_rows
    core_copies = []
    for n, (i, j) in enumerate(offsets + [(0, 0)]):
        q = plane_at(i, j)[0]
        copy = pltpu.make_async_remote_copy(
            src_ref=acc.at[rows_of(give, q)],
            dst_ref=core_in.at[rows_of(0, q)],
            send_sem=core_send.at[n],
            recv_sem=core_recv.at[n],
            device_id=other,
        )
        copy.start()
        core_copies.append(copy)
    plane_copies = []
    for n, (i, j) in enumerate(offsets):
        q, device = plane_at(i, j)
        core_copies[n].wait_recv()
        half[rows_of(0, q), :] = acc[rows_of(keep, q), :] + core_in[rows_of(0, q), :]
        copy = pltpu.make_async_remote_copy(
            src_ref=half.at[rows_of(0, q)],
            dst_ref=plane_in.at[n],
            send_sem=plane_send.at[n],
            recv_sem=plane_recv.at[n],
            device_id=device,
        )
        copy.start()
        plane_copies.append(copy)
    core_copies[-1].wait_recv()
    total = acc[rows_of(keep, p), :] + core_in[rows_of(0, p), :]
    for n in reversed(range(len(offsets))):
        plane_copies[n].wait_recv()
        total = total + plane_in[n]
    mine[...] = total

    spread = nz // tiles
    keepers = [(t * spread % nz, (t * spread + nz // 2) % nz) for t in range(tiles)]
    assert len({v for pair in keepers for v in pair}) == 2 * tiles
    reach = sorted((k for k in range(1 - nz // 4, nz // 4 + 1) if k), key=lambda k: -ring(nz, k))
    distances = sorted(range(1, nz), key=lambda k: ring(nz, k))
    keeps = [(z == a) | (z == b) for a, b in keepers]
    keeper = functools.reduce(lambda v, w: v | w, keeps)
    tile = sum(t * keeps[t].astype(jnp.int32) for t in range(tiles))

    def z_copy(t, m):
        return pltpu.make_async_remote_copy(
            src_ref=mine.at[pl.ds(t * 8, 8)],
            dst_ref=z_in.at[z],
            send_sem=z_send.at[t, m],
            recv_sem=z_recv.at[z],
            device_id={"gx": keepers[t][m]},
        )

    def zg_copy(i, t):
        return pltpu.make_async_remote_copy(
            src_ref=z_sum.at[t],
            dst_ref=z_sum.at[t],
            send_sem=zg_send.at[i],
            recv_sem=zg_recv.at[t],
            device_id=at_z(reach[i]),
        )

    for t in range(tiles):
        for m in (0, 1):

            @pl.when(z != keepers[t][m])
            def _():
                z_copy(t, m).start()

    @pl.when(keeper)
    def _():
        z_in[z] = mine[pl.ds(pl.multiple_of(tile * 8, 8), 8), :]
        for k in distances:
            w = lax.rem(z + k, nz)
            pltpu.make_async_remote_copy(
                src_ref=z_in.at[w],
                dst_ref=z_in.at[w],
                send_sem=z_send.at[0, 0],
                recv_sem=z_recv.at[w],
                device_id={"gx": w},
            ).wait_recv()
        total = z_in[0]
        for w in range(1, nz):
            total = total + z_in[w]
        z_sum[tile] = total * jnp.float32(1.0 / total_rows)
        for i in range(len(reach)):
            zg_copy(i, tile).start()

    for t in range(tiles):

        @pl.when(jnp.logical_not(keeps[t]))
        def _():
            zg_copy(0, t).wait_recv()

    sums[c, p] = z_sum[...].reshape(piece, LANES)

    def cg_copy(n, q):
        return pltpu.make_async_remote_copy(
            src_ref=sums.at[c, q],
            dst_ref=sums.at[c, q],
            send_sem=cg_send.at[n],
            recv_sem=cg_recv.at[n],
            device_id=other,
        )

    pg_copies, cg_copies = [], []
    for n, (i, j) in enumerate(offsets):
        copy = pltpu.make_async_remote_copy(
            src_ref=sums.at[c, p],
            dst_ref=sums.at[c, p],
            send_sem=pg_send.at[n],
            recv_sem=pg_recv.at[n],
            device_id=plane_at(i, j)[1],
        )
        copy.start()
        pg_copies.append(copy)
    cg_copies.append(cg_copy(len(offsets), p))
    cg_copies[-1].start()
    for n in reversed(range(len(offsets))):
        i, j = offsets[n]
        pg_copies[n].wait_recv()
        cg_copies.append(cg_copy(n, plane_at(-i, -j)[0]))
        cg_copies[-1].start()

    for copy in sends + core_copies + plane_copies + pg_copies:
        copy.wait_send()
    for t in range(tiles):
        for m in (0, 1):

            @pl.when(z != keepers[t][m])
            def _():
                z_copy(t, m).wait_send()

    @pl.when(keeper)
    def _():
        for i in range(len(reach)):
            zg_copy(i, tile).wait_send()

    for copy in cg_copies:
        copy.wait()


def reciprocal(d):
    r = pl.reciprocal(d, approx=True)
    return r * (2.0 - d * r)


def short_dot(a, b, ca, cb):
    return lax.dot_general(a, b, (((ca,), (cb,)), ((), ())), preferred_element_type=jnp.float32)


def split(v):
    high = v.astype(jnp.bfloat16)
    rest = v - high.astype(jnp.float32)
    middle = rest.astype(jnp.bfloat16)
    return high, middle, (rest - middle.astype(jnp.float32)).astype(jnp.bfloat16)


def left(v, axis):
    h, m, t = split(v)
    return jnp.concatenate([h, h, m, m, h, t], axis=axis)


def right(v, axis):
    h, m, t = split(v)
    return jnp.concatenate([h, m, h, m, t, h], axis=axis)


def row(v, i):
    return jnp.broadcast_to(v[i : i + 1, :], (8, v.shape[1]))


def inverse_lower(inner):
    rank = inner.shape[0]
    count, groups = rank // PANEL, PANEL // 8
    row8 = lax.broadcasted_iota(jnp.int32, (8, rank), 0)
    lane8 = lax.broadcasted_iota(jnp.int32, (8, rank), 1)
    row_of = lax.broadcasted_iota(jnp.int32, (PANEL, rank), 0)
    lane_of = lax.broadcasted_iota(jnp.int32, (PANEL, rank), 1)
    rest = [inner[t * PANEL : (t + 1) * PANEL] for t in range(count)]
    result = []
    for s in range(count):
        j0, j1 = s * PANEL, (s + 1) * PANEL
        panel = [rest[s][8 * g : 8 * g + 8, :] for g in range(groups)]
        done = {}
        for g0 in range(0, groups, BLOCK // 8):
            c0 = j0 + 8 * g0
            cols = {}
            for k in range(BLOCK):
                for g in range(g0 + k // 8, groups):
                    cols[k, g] = jnp.broadcast_to(panel[g][:, c0 + k : c0 + k + 1], (8, rank))

            def at(j, k):
                return row(cols[j, g0 + k // 8], k % 8)

            p, q, r = at(0, 0), at(0, 1), at(1, 1)
            for j in range(0, BLOCK, 2):
                gj, ij = g0 + j // 8, j % 8
                column = c0 + j
                det = p * r - q * q
                inv = reciprocal(det)
                following = None
                if j + 2 < BLOCK:
                    k = j + 2
                    u1, u2, v1, v2 = at(j, k), at(j + 1, k), at(j, k + 1), at(j + 1, k + 1)
                    a1, a2 = r * u1 - q * u2, p * u2 - q * u1
                    e1, e2 = r * v1 - q * v2, p * v2 - q * v1
                    following = (
                        at(k, k) - (a1 * u1 + a2 * u2) * inv,
                        at(k, k + 1) - (a1 * v1 + a2 * v2) * inv,
                        at(k + 1, k + 1) - (e1 * v1 + e2 * v2) * inv,
                    )
                pi, qi, ri = p * inv, q * inv, r * inv
                first = gj + 1 if ij == 6 else gj
                m1 = {g: cols[j, g] * ri - cols[j + 1, g] * qi for g in range(first, groups)}
                m2 = {g: cols[j + 1, g] * pi - cols[j, g] * qi for g in range(first, groups)}
                for k in range(j + 2, BLOCK):
                    w1, w2 = at(j, k), at(j + 1, k)
                    for g in range(g0 + k // 8, groups):
                        cols[k, g] = cols[k, g] - (m1[g] * w1 + m2[g] * w2)
                here = lane8 // 2 == column // 2
                row1 = jnp.where(here, jnp.where(lane8 == column, 1.0, 0.0), row(panel[gj], ij))
                row2 = jnp.where(here, jnp.where(lane8 == column, 0.0, 1.0), row(panel[gj], ij + 1))
                inv_p = reciprocal(p)
                done[8 * gj + ij] = row1 * lax.rsqrt(p)
                done[8 * gj + ij + 1] = (row2 - (q * inv_p) * row1) * lax.rsqrt(det * inv_p)
                for g in range(first, groups):
                    panel[g] = jnp.where(here, 0.0, panel[g]) - (m1[g] * row1 + m2[g] * row2)
                if following:
                    p, q, r = following
        upper = []
        for g in range(groups):
            v = done[8 * g]
            for i in range(1, 8):
                v = jnp.where(row8 == i, done[8 * g + i], v)
            upper.append(v)
        upper = jnp.concatenate(upper, axis=0)
        lower = lane_of <= row_of + j0
        result.append(jnp.where(lower, upper, 0.0))
        if s + 1 < count:
            kept = jnp.where(lower | (lane_of >= j1), upper, 0.0)
            change = short_dot(left(upper, 0)[:, j1:], right(kept, 0), 0, 0)
            block = (lane_of >= j0) & (lane_of < j1)
            for t in range(s + 1, count):
                part = change[(t - s - 1) * PANEL : (t - s) * PANEL]
                rest[t] = jnp.where(block, 0.0, rest[t]) - part
    return jnp.concatenate(result, axis=0)


def factor_kernel(fib, sums, core, factor, gram):
    blocks = fib.shape[0]
    width = blocks * LANES
    pairs = block_pairs(blocks)
    part = [sums[n * LANES : (n + 1) * LANES, :] for n in range(len(pairs))]
    for n, (i, j) in enumerate(pairs):
        gram[i * LANES : (i + 1) * LANES, j * LANES : (j + 1) * LANES] = part[n]
        if i != j:
            gram[j * LANES : (j + 1) * LANES, i * LANES : (i + 1) * LANES] = part[n].T
    grown_t = jnp.concatenate(part[:blocks], axis=1)
    for step in range(ITERS):
        inner = full_dot(grown_t, grown_t, 1, 1)
        if step < ITERS - 1:
            ready = right(full_dot(grown_t, gram[...], 1, 0), 0)
            grown_t = short_dot(left(inverse_lower(inner), 1), ready, 1, 0)
        else:
            rows = jnp.concatenate([fib[b].reshape(-1, LANES) for b in range(blocks)], axis=1)
            ready = left(jnp.concatenate([grown_t.T, full_dot(rows, grown_t, 1, 1)], axis=0), 1)
            both = short_dot(ready, right(inverse_lower(inner), 1), 1, 1)
            factor[...] = both[:width]
            core[...] = both[width:]


def on_device(sizes, field):
    nz, nx, ny = sizes
    steps, width_x, width_y, width_z = field.shape
    cells = width_y // ny
    width = width_z * ny
    planes = nx * ny
    rows = steps * width_x * cells
    pair_rows = len(block_pairs(ny)) * LANES
    half = pair_rows // 2
    piece = half // planes
    tiles = piece // 8
    f32 = jnp.float32
    dma = pltpu.SemaphoreType.DMA
    fib, sums = pl.pallas_call(
        functools.partial(gather_kernel, sizes, rows * nz * nx * 2 * ny),
        out_shape=(
            jax.ShapeDtypeStruct((ny, steps, width_x, cells, width_z), f32),
            jax.ShapeDtypeStruct((2, planes, piece, LANES), f32),
        ),
        in_specs=[pl.BlockSpec(memory_space=pl.ANY)],
        out_specs=(VMEM, VMEM),
        scratch_shapes=[
            pltpu.VMEM((pair_rows, LANES), f32),
            pltpu.VMEM((half, LANES), f32),
            pltpu.VMEM((half, LANES), f32),
            pltpu.VMEM((planes - 1, piece, LANES), f32),
            pltpu.VMEM((piece, LANES), f32),
            pltpu.VMEM((nz, 8, LANES), f32),
            pltpu.VMEM((tiles, 8, LANES), f32),
            pltpu.SemaphoreType.REGULAR((3,)),
            dma((2*steps,)),
            dma((2*steps, ny - 1)),
            dma((2*steps, ny - 1)),
            dma((planes,)),
            dma((planes,)),
            dma((planes - 1,)),
            dma((planes - 1,)),
            dma((tiles, 2)),
            dma((nz,)),
            dma((nz // 2 - 1,)),
            dma((tiles,)),
            dma((planes - 1,)),
            dma((planes - 1,)),
            dma((planes,)),
            dma((planes,)),
        ],
        compiler_params=pltpu.CompilerParams(
            collective_id=0, has_side_effects=True, vmem_limit_bytes=24 * 2**20
        ),
        name="gather_gram",
    )(field)
    core, factor = pl.pallas_call(
        factor_kernel,
        out_shape=(
            jax.ShapeDtypeStruct((rows, RANK), f32),
            jax.ShapeDtypeStruct((width, RANK), f32),
        ),
        in_specs=[VMEM, VMEM],
        out_specs=(VMEM, VMEM),
        scratch_shapes=[
            pltpu.VMEM((width, width), f32),
        ],
        compiler_params=pltpu.CompilerParams(vmem_limit_bytes=24 * 2**20),
        name="factor_core",
    )(fib, sums.reshape(pair_rows, LANES))
    return core.reshape(steps, width_x, cells, RANK), factor


def solution(mesh):
    sizes = (mesh.shape["gx"], mesh.shape["gy"] // 2, mesh.shape["gz"])
    return jax.shard_map(
        functools.partial(on_device, sizes),
        mesh=mesh,
        in_specs=(P(None, "gx", "gy", "gz"),),
        out_specs=(P(None, "gx", ("gy", "gz"), None), P()),
        check_vma=False,
    )
```

```python
import functools

import jax
import jax.numpy as jnp
from jax import lax
from jax.experimental import pallas as pl
from jax.experimental.pallas import tpu as pltpu
from jax.sharding import PartitionSpec as P

RANK = 128
ITERS = 4
LANES = 128
PANEL = 32
BLOCK = 16
VMEM = pl.BlockSpec(memory_space=pltpu.VMEM)


def full_dot(a, b, ca, cb):
    return lax.dot_general(
        a,
        b,
        (((ca,), (cb,)), ((), ())),
        precision=lax.Precision.HIGHEST,
        preferred_element_type=jnp.float32,
    )


def block_pairs(blocks):
    return [(i, j) for i in range(blocks) for j in range(i, blocks)]


def ring(n, k):
    return min(k % n, -k % n)


def gather_kernel(
    sizes, total_rows, field, fib, sums, acc, half, core_in, plane_in, mine, z_in, z_sum,
    known, own_sem, a2a_send, a2a_recv, core_send, core_recv, plane_send, plane_recv, z_send, z_recv,
    zg_send, zg_recv, pg_send, pg_recv, cg_send, cg_recv,
):
    nz, nx, ny = sizes
    planes = nx * ny
    blocks = ny
    pairs = block_pairs(blocks)
    cells = fib.shape[3]
    steps = fib.shape[1]
    half_rows = half.shape[0]
    piece = plane_in.shape[1]
    tiles = piece // 8
    z = lax.axis_index("gx")
    gy = lax.axis_index("gy")
    x = gy // 2
    c = gy % 2
    y = lax.axis_index("gz")
    p = x * ny + y

    def at_x(k):
        return {"gy": lax.rem(x + k % nx, nx) * 2 + c}

    def at_y(k):
        return {"gz": lax.rem(y + k % ny, ny)}

    def at_z(k):
        return {"gx": lax.rem(z + k % nz, nz)}

    other = {"gy": x * 2 + (1 - c)}

    def arrived(ref, sem):
        pltpu.make_async_remote_copy(
            src_ref=ref, dst_ref=ref, send_sem=sem, recv_sem=sem, device_id=other
        ).wait_recv()

    def left_here(ref, sem):
        pltpu.make_async_remote_copy(
            src_ref=ref, dst_ref=ref, send_sem=sem, recv_sem=sem, device_id=other
        ).wait_send()

    barrier = pltpu.get_barrier_semaphore()
    near = [at_y(k) for k in range(1, ny)] + [other, at_x(1), at_x(-1), at_z(1), at_z(-1)]
    for device in near:
        pl.semaphore_signal(barrier, inc=1, device_id=device)
    pl.semaphore_wait(barrier, len(near))

    deep = fib.shape[2] // 2
    chunks = [(s, pl.ds(h * deep, deep)) for s in range(steps) for h in range(2)]
    order = sorted(range(1, ny), key=lambda k: -ring(ny, k))
    for n, (s, part) in enumerate(chunks):
        for k in order:
            to = lax.rem(y + k, ny)
            copy = pltpu.make_async_remote_copy(
                src_ref=field.at[s, part, pl.ds(to * cells, cells), :],
                dst_ref=fib.at[y, s, part],
                send_sem=a2a_send,
                recv_sem=a2a_recv.at[n],
                device_id={"gz": to},
            )
            copy.start()
    owns = []
    for n, (s, part) in enumerate(chunks):
        copy = pltpu.make_async_copy(
            field.at[s, part, pl.ds(y * cells, cells), :], fib.at[y, s, part], own_sem.at[n]
        )
        copy.start()
        owns.append(copy)

    rounds = [[at_x(1), at_x(-1), at_z(1), at_z(-1)], [at_z(2), at_z(-2)], [at_z(4), at_z(-4)]]
    if nx > 2:
        rounds[1].append(at_x(2))
    for i, devices in enumerate(rounds):
        for device in devices:
            pl.semaphore_signal(known.at[i], inc=1, device_id=device)
        pl.semaphore_wait(known.at[i], len(devices))

    for n, (s, part) in enumerate(chunks):
        owns[n].wait()
        arrived(fib.at[pl.ds(0, ny - 1), s, part], a2a_recv.at[n])
        x0 = (n % 2) * deep
        rows = jnp.concatenate([fib[b, s, x0 : x0 + deep].reshape(-1, LANES) for b in range(blocks)], axis=1)
        for i in range(0, blocks, 2):
            term = full_dot(rows[:, i * LANES : (i + 2) * LANES], rows[:, i * LANES :], 0, 0)
            for a in (0, 1):
                for b in range(i + a, blocks):
                    r = pairs.index((i + a, b)) * LANES
                    part = term[a * LANES : (a + 1) * LANES, (b - i) * LANES : (b - i + 1) * LANES]
                    if n == 0:
                        acc[r : r + LANES, :] = part
                    else:
                        acc[r : r + LANES, :] = acc[r : r + LANES, :] + part

    offsets = [(i, j) for i in range(nx) for j in range(ny) if (i, j) != (0, 0)]
    offsets.sort(key=lambda o: -(ring(nx, o[0]) + ring(ny, o[1])))

    def plane_at(i, j):
        to_x, to_y = lax.rem(x + i % nx, nx), lax.rem(y + j % ny, ny)
        return to_x * ny + to_y, {"gy": to_x * 2 + c, "gz": to_y}

    def rows_of(start, q):
        return pl.ds(pl.multiple_of(start + q * piece, 8), piece)

    hops = [ring(nx, i) + ring(ny, j) for i, j in offsets] + [0]
    groups = [[n for n in range(planes) if hops[n] == h] for h in range(max(hops), -1, -1)]
    keep = c * half_rows
    give = (1 - c) * half_rows
    for n, (i, j) in enumerate(offsets + [(0, 0)]):
        q = plane_at(i, j)[0]
        copy = pltpu.make_async_remote_copy(
            src_ref=acc.at[rows_of(give, q)],
            dst_ref=core_in.at[rows_of(0, q)],
            send_sem=core_send,
            recv_sem=core_recv.at[hops[0] - hops[n]],
            device_id=other,
        )
        copy.start()
    for n, (i, j) in enumerate(offsets):
        q, device = plane_at(i, j)
        h = hops[0] - hops[n]
        if n == groups[h][0]:
            arrived(core_in.at[pl.ds(0, len(groups[h]) * piece)], core_recv.at[h])
        half[rows_of(0, q), :] = acc[rows_of(keep, q), :] + core_in[rows_of(0, q), :]
        copy = pltpu.make_async_remote_copy(
            src_ref=half.at[rows_of(0, q)],
            dst_ref=plane_in.at[n],
            send_sem=plane_send,
            recv_sem=plane_recv,
            device_id=device,
        )
        copy.start()
    arrived(core_in.at[pl.ds(0, piece)], core_recv.at[len(groups) - 1])
    total = acc[rows_of(keep, p), :] + core_in[rows_of(0, p), :]
    arrived(plane_in, plane_recv)
    for n in range(len(offsets)):
        total = total + plane_in[n]
    mine[...] = total

    spread = nz // tiles
    keepers = [(t * spread % nz, (t * spread + nz // 2) % nz) for t in range(tiles)]
    assert len({v for pair in keepers for v in pair}) == 2 * tiles
    reach = sorted((k for k in range(1 - nz // 4, nz // 4 + 1) if k), key=lambda k: -ring(nz, k))
    keeps = [(z == a) | (z == b) for a, b in keepers]
    keeper = functools.reduce(lambda v, w: v | w, keeps)
    tile = sum(t * keeps[t].astype(jnp.int32) for t in range(tiles))

    def z_copy(t, m):
        return pltpu.make_async_remote_copy(
            src_ref=mine.at[pl.ds(t * 8, 8)],
            dst_ref=z_in.at[z],
            send_sem=z_send,
            recv_sem=z_recv,
            device_id={"gx": keepers[t][m]},
        )

    def zg_copy(i, t):
        return pltpu.make_async_remote_copy(
            src_ref=z_sum.at[t],
            dst_ref=z_sum.at[t],
            send_sem=zg_send,
            recv_sem=zg_recv.at[t],
            device_id=at_z(reach[i]),
        )

    for t in range(tiles):
        for m in (0, 1):

            @pl.when(z != keepers[t][m])
            def _():
                z_copy(t, m).start()

    @pl.when(keeper)
    def _():
        z_in[z] = mine[pl.ds(pl.multiple_of(tile * 8, 8), 8), :]
        arrived(z_in.at[pl.ds(0, nz - 1)], z_recv)
        total = z_in[0]
        for w in range(1, nz):
            total = total + z_in[w]
        z_sum[tile] = total * jnp.float32(1.0 / total_rows)
        for i in range(len(reach)):
            zg_copy(i, tile).start()

    for t in range(tiles):

        @pl.when(jnp.logical_not(keeps[t]))
        def _():
            zg_copy(0, t).wait_recv()

    sums[c, p] = z_sum[...].reshape(piece, LANES)

    def cg_copy(q):
        return pltpu.make_async_remote_copy(
            src_ref=sums.at[c, q],
            dst_ref=sums.at[c, q],
            send_sem=cg_send,
            recv_sem=cg_recv,
            device_id=other,
        )

    for n, (i, j) in enumerate(offsets):
        pltpu.make_async_remote_copy(
            src_ref=sums.at[c, p],
            dst_ref=sums.at[c, p],
            send_sem=pg_send,
            recv_sem=pg_recv.at[hops[0] - hops[n]],
            device_id=plane_at(i, j)[1],
        ).start()
    cg_copy(p).start()
    for h in reversed(range(len(groups) - 1)):
        arrived(sums.at[0, pl.ds(0, len(groups[h]))], pg_recv.at[h])
        for n in groups[h]:
            i, j = offsets[n]
            cg_copy(plane_at(-i, -j)[0]).start()

    left_here(fib.at[pl.ds(0, ny - 1)], a2a_send)
    left_here(acc.at[pl.ds(0, half_rows)], core_send)
    left_here(half.at[pl.ds(0, half_rows - piece)], plane_send)
    left_here(sums.at[0, pl.ds(0, planes - 1)], pg_send)

    @pl.when(keeper)
    def _():
        left_here(z_in.at[pl.ds(0, 2 * tiles - 1)], z_send)
        left_here(z_in.at[pl.ds(0, len(reach))], zg_send)

    @pl.when(jnp.logical_not(keeper))
    def _():
        left_here(z_in.at[pl.ds(0, 2 * tiles)], z_send)

    left_here(sums.at[0], cg_send)
    arrived(sums.at[0], cg_recv)


def reciprocal(d):
    r = pl.reciprocal(d, approx=True)
    return r * (2.0 - d * r)


def short_dot(a, b, ca, cb):
    return lax.dot_general(a, b, (((ca,), (cb,)), ((), ())), preferred_element_type=jnp.float32)


def split(v):
    high = v.astype(jnp.bfloat16)
    rest = v - high.astype(jnp.float32)
    middle = rest.astype(jnp.bfloat16)
    return high, middle, (rest - middle.astype(jnp.float32)).astype(jnp.bfloat16)


def left(v, axis):
    h, m, t = split(v)
    return jnp.concatenate([h, h, m, m, h, t], axis=axis)


def right(v, axis):
    h, m, t = split(v)
    return jnp.concatenate([h, m, h, m, t, h], axis=axis)


def row(v, i):
    return jnp.broadcast_to(v[i : i + 1, :], (8, v.shape[1]))


def inverse_lower(inner):
    rank = inner.shape[0]
    count, groups = rank // PANEL, PANEL // 8
    row8 = lax.broadcasted_iota(jnp.int32, (8, rank), 0)
    lane8 = lax.broadcasted_iota(jnp.int32, (8, rank), 1)
    row_of = lax.broadcasted_iota(jnp.int32, (PANEL, rank), 0)
    lane_of = lax.broadcasted_iota(jnp.int32, (PANEL, rank), 1)
    rest = [inner[t * PANEL : (t + 1) * PANEL] for t in range(count)]
    result = []
    for s in range(count):
        j0, j1 = s * PANEL, (s + 1) * PANEL
        panel = [rest[s][8 * g : 8 * g + 8, :] for g in range(groups)]
        done = {}
        for g0 in range(0, groups, BLOCK // 8):
            c0 = j0 + 8 * g0
            cols = {}
            for k in range(BLOCK):
                for g in range(g0 + k // 8, groups):
                    cols[k, g] = jnp.broadcast_to(panel[g][:, c0 + k : c0 + k + 1], (8, rank))

            def at(j, k):
                return row(cols[j, g0 + k // 8], k % 8)

            p, q, r = at(0, 0), at(0, 1), at(1, 1)
            for j in range(0, BLOCK, 2):
                gj, ij = g0 + j // 8, j % 8
                column = c0 + j
                det = p * r - q * q
                inv = reciprocal(det)
                following = None
                if j + 2 < BLOCK:
                    k = j + 2
                    u1, u2, v1, v2 = at(j, k), at(j + 1, k), at(j, k + 1), at(j + 1, k + 1)
                    a1, a2 = r * u1 - q * u2, p * u2 - q * u1
                    e1, e2 = r * v1 - q * v2, p * v2 - q * v1
                    following = (
                        at(k, k) - (a1 * u1 + a2 * u2) * inv,
                        at(k, k + 1) - (a1 * v1 + a2 * v2) * inv,
                        at(k + 1, k + 1) - (e1 * v1 + e2 * v2) * inv,
                    )
                pi, qi, ri = p * inv, q * inv, r * inv
                first = gj + 1 if ij == 6 else gj
                m1 = {g: cols[j, g] * ri - cols[j + 1, g] * qi for g in range(first, groups)}
                m2 = {g: cols[j + 1, g] * pi - cols[j, g] * qi for g in range(first, groups)}
                for k in range(j + 2, BLOCK):
                    w1, w2 = at(j, k), at(j + 1, k)
                    for g in range(g0 + k // 8, groups):
                        cols[k, g] = cols[k, g] - (m1[g] * w1 + m2[g] * w2)
                here = lane8 // 2 == column // 2
                row1 = jnp.where(here, jnp.where(lane8 == column, 1.0, 0.0), row(panel[gj], ij))
                row2 = jnp.where(here, jnp.where(lane8 == column, 0.0, 1.0), row(panel[gj], ij + 1))
                inv_p = reciprocal(p)
                done[8 * gj + ij] = row1 * lax.rsqrt(p)
                done[8 * gj + ij + 1] = (row2 - (q * inv_p) * row1) * lax.rsqrt(det * inv_p)
                for g in range(first, groups):
                    panel[g] = jnp.where(here, 0.0, panel[g]) - (m1[g] * row1 + m2[g] * row2)
                if following:
                    p, q, r = following
        upper = []
        for g in range(groups):
            v = done[8 * g]
            for i in range(1, 8):
                v = jnp.where(row8 == i, done[8 * g + i], v)
            upper.append(v)
        upper = jnp.concatenate(upper, axis=0)
        lower = lane_of <= row_of + j0
        result.append(jnp.where(lower, upper, 0.0))
        if s + 1 < count:
            kept = jnp.where(lower | (lane_of >= j1), upper, 0.0)
            change = short_dot(left(upper, 0)[:, j1:], right(kept, 0), 0, 0)
            block = (lane_of >= j0) & (lane_of < j1)
            for t in range(s + 1, count):
                part = change[(t - s - 1) * PANEL : (t - s) * PANEL]
                rest[t] = jnp.where(block, 0.0, rest[t]) - part
    return jnp.concatenate(result, axis=0)


def factor_kernel(fib, sums, core, factor, gram):
    blocks = fib.shape[0]
    width = blocks * LANES
    pairs = block_pairs(blocks)
    part = [sums[n * LANES : (n + 1) * LANES, :] for n in range(len(pairs))]
    for n, (i, j) in enumerate(pairs):
        gram[i * LANES : (i + 1) * LANES, j * LANES : (j + 1) * LANES] = part[n]
        if i != j:
            gram[j * LANES : (j + 1) * LANES, i * LANES : (i + 1) * LANES] = part[n].T
    grown_t = jnp.concatenate(part[:blocks], axis=1)
    for step in range(ITERS):
        inner = full_dot(grown_t, grown_t, 1, 1)
        if step < ITERS - 1:
            ready = right(full_dot(grown_t, gram[...], 1, 0), 0)
            grown_t = short_dot(left(inverse_lower(inner), 1), ready, 1, 0)
        else:
            rows = jnp.concatenate([fib[b].reshape(-1, LANES) for b in range(blocks)], axis=1)
            ready = left(jnp.concatenate([grown_t.T, full_dot(rows, grown_t, 1, 1)], axis=0), 1)
            both = short_dot(ready, right(inverse_lower(inner), 1), 1, 1)
            factor[...] = both[:width]
            core[...] = both[width:]


def on_device(sizes, field):
    nz, nx, ny = sizes
    steps, width_x, width_y, width_z = field.shape
    cells = width_y // ny
    width = width_z * ny
    planes = nx * ny
    rows = steps * width_x * cells
    pair_rows = len(block_pairs(ny)) * LANES
    half = pair_rows // 2
    piece = half // planes
    tiles = piece // 8
    f32 = jnp.float32
    dma = pltpu.SemaphoreType.DMA
    fib, sums = pl.pallas_call(
        functools.partial(gather_kernel, sizes, rows * nz * nx * 2 * ny),
        out_shape=(
            jax.ShapeDtypeStruct((ny, steps, width_x, cells, width_z), f32),
            jax.ShapeDtypeStruct((2, planes, piece, LANES), f32),
        ),
        in_specs=[pl.BlockSpec(memory_space=pl.ANY)],
        out_specs=(VMEM, VMEM),
        scratch_shapes=[
            pltpu.VMEM((pair_rows, LANES), f32),
            pltpu.VMEM((half, LANES), f32),
            pltpu.VMEM((half, LANES), f32),
            pltpu.VMEM((planes - 1, piece, LANES), f32),
            pltpu.VMEM((piece, LANES), f32),
            pltpu.VMEM((nz, 8, LANES), f32),
            pltpu.VMEM((tiles, 8, LANES), f32),
            pltpu.SemaphoreType.REGULAR((3,)),
            dma((2 * steps,)),
            dma,
            dma((2 * steps,)),
            dma,
            dma((nx // 2 + ny // 2 + 1,)),
            dma,
            dma,
            dma,
            dma,
            dma,
            dma((tiles,)),
            dma,
            dma((nx // 2 + ny // 2,)),
            dma,
            dma,
        ],
        compiler_params=pltpu.CompilerParams(
            collective_id=0, has_side_effects=True, vmem_limit_bytes=52 * 2**20
        ),
        name="gather_gram",
    )(field)
    core, factor = pl.pallas_call(
        factor_kernel,
        out_shape=(
            jax.ShapeDtypeStruct((rows, RANK), f32),
            jax.ShapeDtypeStruct((width, RANK), f32),
        ),
        in_specs=[VMEM, VMEM],
        out_specs=(VMEM, VMEM),
        scratch_shapes=[
            pltpu.VMEM((width, width), f32),
        ],
        compiler_params=pltpu.CompilerParams(vmem_limit_bytes=24 * 2**20),
        name="factor_core",
    )(fib, sums.reshape(pair_rows, LANES))
    return core.reshape(steps, width_x, cells, RANK), factor


def solution(mesh):
    sizes = (mesh.shape["gx"], mesh.shape["gy"] // 2, mesh.shape["gz"])
    return jax.shard_map(
        functools.partial(on_device, sizes),
        mesh=mesh,
        in_specs=(P(None, "gx", "gy", "gz"),),
        out_specs=(P(None, "gx", ("gy", "gz"), None), P()),
        check_vma=False,
    )
```

```python
import functools

import jax
import jax.numpy as jnp
from jax import lax
from jax.experimental import pallas as pl
from jax.experimental.pallas import tpu as pltpu
from jax.sharding import PartitionSpec as P

RANK = 128
ITERS = 4
LANES = 128
PANEL = 32
BLOCK = 16
VMEM = pl.BlockSpec(memory_space=pltpu.VMEM)


def full_dot(a, b, ca, cb):
    return lax.dot_general(
        a,
        b,
        (((ca,), (cb,)), ((), ())),
        precision=lax.Precision.HIGHEST,
        preferred_element_type=jnp.float32,
    )


def block_pairs(blocks):
    return [(i, j) for i in range(blocks) for j in range(i, blocks)]


def ring(n, k):
    return min(k % n, -k % n)


def gather_kernel(
    sizes, total_rows, field, fib, sums, acc, half, core_in, plane_in, mine, z_in, z_sum,
    known, own_sem, a2a_send, a2a_recv, core_send, core_recv, plane_send, plane_recv, z_send, z_recv,
    zg_send, zg_recv, pg_send, pg_recv, cg_send, cg_recv,
):
    nz, nx, ny = sizes
    planes = nx * ny
    blocks = ny
    pairs = block_pairs(blocks)
    cells = fib.shape[3]
    steps = fib.shape[1]
    half_rows = half.shape[0]
    piece = plane_in.shape[1]
    tiles = piece // 8
    z = lax.axis_index("gx")
    gy = lax.axis_index("gy")
    x = gy // 2
    c = gy % 2
    y = lax.axis_index("gz")
    p = x * ny + y

    def at_x(k):
        return {"gy": lax.rem(x + k % nx, nx) * 2 + c}

    def at_y(k):
        return {"gz": lax.rem(y + k % ny, ny)}

    def at_z(k):
        return {"gx": lax.rem(z + k % nz, nz)}

    other = {"gy": x * 2 + (1 - c)}

    def arrived(ref, sem):
        pltpu.make_async_remote_copy(
            src_ref=ref, dst_ref=ref, send_sem=sem, recv_sem=sem, device_id=other
        ).wait_recv()

    def left_here(ref, sem):
        pltpu.make_async_remote_copy(
            src_ref=ref, dst_ref=ref, send_sem=sem, recv_sem=sem, device_id=other
        ).wait_send()

    deep = fib.shape[2] // 2
    chunks = [(s, pl.ds(h * deep, deep)) for s in range(steps) for h in range(2)]
    owns = []
    for n, (s, part) in enumerate(chunks):
        copy = pltpu.make_async_copy(
            field.at[s, part, pl.ds(y * cells, cells), :], fib.at[y, s, part], own_sem.at[n]
        )
        copy.start()
        owns.append(copy)

    barrier = pltpu.get_barrier_semaphore()
    near = [at_y(k) for k in range(1, ny)] + [other, at_x(1), at_x(-1), at_z(1), at_z(-1)]
    for device in near:
        pl.semaphore_signal(barrier, inc=1, device_id=device)
    pl.semaphore_wait(barrier, len(near))

    order = sorted(range(1, ny), key=lambda k: ring(ny, k))
    for n, (s, part) in enumerate(chunks):
        for k in order:
            to = lax.rem(y + k, ny)
            copy = pltpu.make_async_remote_copy(
                src_ref=field.at[s, part, pl.ds(to * cells, cells), :],
                dst_ref=fib.at[y, s, part],
                send_sem=a2a_send,
                recv_sem=a2a_recv.at[n],
                device_id={"gz": to},
            )
            copy.start()
    rounds = [[at_x(1), at_x(-1), at_z(1), at_z(-1)], [at_z(2), at_z(-2)], [at_z(4), at_z(-4)]]
    if nx > 2:
        rounds[1].append(at_x(2))
    for i, devices in enumerate(rounds):
        for device in devices:
            pl.semaphore_signal(known.at[i], inc=1, device_id=device)
        pl.semaphore_wait(known.at[i], len(devices))

    for n, (s, part) in enumerate(chunks):
        owns[n].wait()
        arrived(fib.at[pl.ds(0, ny - 1), s, part], a2a_recv.at[n])
        x0 = (n % 2) * deep
        rows = jnp.concatenate([fib[b, s, x0 : x0 + deep].reshape(-1, LANES) for b in range(blocks)], axis=1)
        lhs, rhs = left(rows, 0), right(rows, 0)
        for i in range(0, blocks, 2):
            term = short_dot(lhs[:, i * LANES : (i + 2) * LANES], rhs[:, i * LANES :], 0, 0)
            for a in (0, 1):
                for b in range(i + a, blocks):
                    r = pairs.index((i + a, b)) * LANES
                    part = term[a * LANES : (a + 1) * LANES, (b - i) * LANES : (b - i + 1) * LANES]
                    if n == 0:
                        acc[r : r + LANES, :] = part
                    else:
                        acc[r : r + LANES, :] = acc[r : r + LANES, :] + part

    offsets = [(i, j) for i in range(nx) for j in range(ny) if (i, j) != (0, 0)]
    offsets.sort(key=lambda o: -(ring(nx, o[0]) + ring(ny, o[1])))

    def plane_at(i, j):
        to_x, to_y = lax.rem(x + i % nx, nx), lax.rem(y + j % ny, ny)
        return to_x * ny + to_y, {"gy": to_x * 2 + c, "gz": to_y}

    def rows_of(start, q):
        return pl.ds(pl.multiple_of(start + q * piece, 8), piece)

    hops = [ring(nx, i) + ring(ny, j) for i, j in offsets] + [0]
    groups = [[n for n in range(planes) if hops[n] == h] for h in range(max(hops), -1, -1)]
    keep = c * half_rows
    give = (1 - c) * half_rows
    for n, (i, j) in enumerate(offsets + [(0, 0)]):
        q = plane_at(i, j)[0]
        copy = pltpu.make_async_remote_copy(
            src_ref=acc.at[rows_of(give, q)],
            dst_ref=core_in.at[rows_of(0, q)],
            send_sem=core_send,
            recv_sem=core_recv.at[hops[0] - hops[n]],
            device_id=other,
        )
        copy.start()
    for n, (i, j) in enumerate(offsets):
        q, device = plane_at(i, j)
        h = hops[0] - hops[n]
        if n == groups[h][0]:
            arrived(core_in.at[pl.ds(0, len(groups[h]) * piece)], core_recv.at[h])
        half[rows_of(0, q), :] = acc[rows_of(keep, q), :] + core_in[rows_of(0, q), :]
        copy = pltpu.make_async_remote_copy(
            src_ref=half.at[rows_of(0, q)],
            dst_ref=plane_in.at[n],
            send_sem=plane_send,
            recv_sem=plane_recv,
            device_id=device,
        )
        copy.start()
    arrived(core_in.at[pl.ds(0, piece)], core_recv.at[len(groups) - 1])
    total = acc[rows_of(keep, p), :] + core_in[rows_of(0, p), :]
    arrived(plane_in, plane_recv)
    for n in range(len(offsets)):
        total = total + plane_in[n]
    mine[...] = total

    spread = nz // tiles
    keepers = [(t * spread % nz, (t * spread + nz // 2) % nz) for t in range(tiles)]
    assert len({v for pair in keepers for v in pair}) == 2 * tiles
    reach = sorted((k for k in range(1 - nz // 4, nz // 4 + 1) if k), key=lambda k: -ring(nz, k))
    keeps = [(z == a) | (z == b) for a, b in keepers]
    keeper = functools.reduce(lambda v, w: v | w, keeps)
    tile = sum(t * keeps[t].astype(jnp.int32) for t in range(tiles))

    def z_copy(t, m):
        return pltpu.make_async_remote_copy(
            src_ref=mine.at[pl.ds(t * 8, 8)],
            dst_ref=z_in.at[z],
            send_sem=z_send,
            recv_sem=z_recv,
            device_id={"gx": keepers[t][m]},
        )

    def zg_copy(i, t):
        return pltpu.make_async_remote_copy(
            src_ref=z_sum.at[t],
            dst_ref=z_sum.at[t],
            send_sem=zg_send,
            recv_sem=zg_recv.at[t],
            device_id=at_z(reach[i]),
        )

    for t in range(tiles):
        for m in (0, 1):

            @pl.when(z != keepers[t][m])
            def _():
                z_copy(t, m).start()

    @pl.when(keeper)
    def _():
        z_in[z] = mine[pl.ds(pl.multiple_of(tile * 8, 8), 8), :]
        arrived(z_in.at[pl.ds(0, nz - 1)], z_recv)
        total = z_in[0]
        for w in range(1, nz):
            total = total + z_in[w]
        z_sum[tile] = total * jnp.float32(1.0 / total_rows)
        for i in range(len(reach)):
            zg_copy(i, tile).start()

    for t in range(tiles):

        @pl.when(jnp.logical_not(keeps[t]))
        def _():
            zg_copy(0, t).wait_recv()

    sums[c, p] = z_sum[...].reshape(piece, LANES)

    def cg_copy(q):
        return pltpu.make_async_remote_copy(
            src_ref=sums.at[c, q],
            dst_ref=sums.at[c, q],
            send_sem=cg_send,
            recv_sem=cg_recv,
            device_id=other,
        )

    for n, (i, j) in enumerate(offsets):
        pltpu.make_async_remote_copy(
            src_ref=sums.at[c, p],
            dst_ref=sums.at[c, p],
            send_sem=pg_send,
            recv_sem=pg_recv.at[hops[0] - hops[n]],
            device_id=plane_at(i, j)[1],
        ).start()
    cg_copy(p).start()
    for h in reversed(range(len(groups) - 1)):
        arrived(sums.at[0, pl.ds(0, len(groups[h]))], pg_recv.at[h])
        for n in groups[h]:
            i, j = offsets[n]
            cg_copy(plane_at(-i, -j)[0]).start()

    left_here(fib.at[pl.ds(0, ny - 1)], a2a_send)
    left_here(acc.at[pl.ds(0, half_rows)], core_send)
    left_here(half.at[pl.ds(0, half_rows - piece)], plane_send)
    left_here(sums.at[0, pl.ds(0, planes - 1)], pg_send)

    @pl.when(keeper)
    def _():
        left_here(z_in.at[pl.ds(0, 2 * tiles - 1)], z_send)
        left_here(z_in.at[pl.ds(0, len(reach))], zg_send)

    @pl.when(jnp.logical_not(keeper))
    def _():
        left_here(z_in.at[pl.ds(0, 2 * tiles)], z_send)

    left_here(sums.at[0], cg_send)
    arrived(sums.at[0], cg_recv)


def reciprocal(d):
    r = pl.reciprocal(d, approx=True)
    return r * (2.0 - d * r)


def short_dot(a, b, ca, cb):
    return lax.dot_general(a, b, (((ca,), (cb,)), ((), ())), preferred_element_type=jnp.float32)


def split(v):
    high = v.astype(jnp.bfloat16)
    rest = v - high.astype(jnp.float32)
    middle = rest.astype(jnp.bfloat16)
    return high, middle, (rest - middle.astype(jnp.float32)).astype(jnp.bfloat16)


def left(v, axis):
    h, m, t = split(v)
    return jnp.concatenate([h, h, m, m, h, t], axis=axis)


def right(v, axis):
    h, m, t = split(v)
    return jnp.concatenate([h, m, h, m, t, h], axis=axis)


def row(v, i):
    return jnp.broadcast_to(v[i : i + 1, :], (8, v.shape[1]))


def inverse_lower(inner):
    rank = inner.shape[0]
    count, groups = rank // PANEL, PANEL // 8
    row8 = lax.broadcasted_iota(jnp.int32, (8, rank), 0)
    lane8 = lax.broadcasted_iota(jnp.int32, (8, rank), 1)
    row_of = lax.broadcasted_iota(jnp.int32, (PANEL, rank), 0)
    lane_of = lax.broadcasted_iota(jnp.int32, (PANEL, rank), 1)
    rest = [inner[t * PANEL : (t + 1) * PANEL] for t in range(count)]
    result = []
    for s in range(count):
        j0, j1 = s * PANEL, (s + 1) * PANEL
        panel = [rest[s][8 * g : 8 * g + 8, :] for g in range(groups)]
        done = {}
        for g0 in range(0, groups, BLOCK // 8):
            c0 = j0 + 8 * g0
            cols = {}
            for k in range(BLOCK):
                for g in range(g0 + k // 8, groups):
                    cols[k, g] = jnp.broadcast_to(panel[g][:, c0 + k : c0 + k + 1], (8, rank))

            def at(j, k):
                return row(cols[j, g0 + k // 8], k % 8)

            p, q, r = at(0, 0), at(0, 1), at(1, 1)
            for j in range(0, BLOCK, 2):
                gj, ij = g0 + j // 8, j % 8
                column = c0 + j
                det = p * r - q * q
                inv = reciprocal(det)
                following = None
                if j + 2 < BLOCK:
                    k = j + 2
                    u1, u2, v1, v2 = at(j, k), at(j + 1, k), at(j, k + 1), at(j + 1, k + 1)
                    a1, a2 = r * u1 - q * u2, p * u2 - q * u1
                    e1, e2 = r * v1 - q * v2, p * v2 - q * v1
                    following = (
                        at(k, k) - (a1 * u1 + a2 * u2) * inv,
                        at(k, k + 1) - (a1 * v1 + a2 * v2) * inv,
                        at(k + 1, k + 1) - (e1 * v1 + e2 * v2) * inv,
                    )
                pi, qi, ri = p * inv, q * inv, r * inv
                first = gj + 1 if ij == 6 else gj
                m1 = {g: cols[j, g] * ri - cols[j + 1, g] * qi for g in range(first, groups)}
                m2 = {g: cols[j + 1, g] * pi - cols[j, g] * qi for g in range(first, groups)}
                for k in range(j + 2, BLOCK):
                    w1, w2 = at(j, k), at(j + 1, k)
                    for g in range(g0 + k // 8, groups):
                        cols[k, g] = cols[k, g] - (m1[g] * w1 + m2[g] * w2)
                here = lane8 // 2 == column // 2
                row1 = jnp.where(here, jnp.where(lane8 == column, 1.0, 0.0), row(panel[gj], ij))
                row2 = jnp.where(here, jnp.where(lane8 == column, 0.0, 1.0), row(panel[gj], ij + 1))
                inv_p = reciprocal(p)
                done[8 * gj + ij] = row1 * lax.rsqrt(p)
                done[8 * gj + ij + 1] = (row2 - (q * inv_p) * row1) * lax.rsqrt(det * inv_p)
                for g in range(first, groups):
                    panel[g] = jnp.where(here, 0.0, panel[g]) - (m1[g] * row1 + m2[g] * row2)
                if following:
                    p, q, r = following
        upper = []
        for g in range(groups):
            v = done[8 * g]
            for i in range(1, 8):
                v = jnp.where(row8 == i, done[8 * g + i], v)
            upper.append(v)
        upper = jnp.concatenate(upper, axis=0)
        lower = lane_of <= row_of + j0
        result.append(jnp.where(lower, upper, 0.0))
        if s + 1 < count:
            kept = jnp.where(lower | (lane_of >= j1), upper, 0.0)
            change = short_dot(left(upper, 0)[:, j1:], right(kept, 0), 0, 0)
            block = (lane_of >= j0) & (lane_of < j1)
            for t in range(s + 1, count):
                part = change[(t - s - 1) * PANEL : (t - s) * PANEL]
                rest[t] = jnp.where(block, 0.0, rest[t]) - part
    return jnp.concatenate(result, axis=0)


def factor_kernel(fib, sums, core, factor, gram):
    blocks = fib.shape[0]
    width = blocks * LANES
    pairs = block_pairs(blocks)
    part = [sums[n * LANES : (n + 1) * LANES, :] for n in range(len(pairs))]
    for n, (i, j) in enumerate(pairs):
        gram[i * LANES : (i + 1) * LANES, j * LANES : (j + 1) * LANES] = part[n]
        if i != j:
            gram[j * LANES : (j + 1) * LANES, i * LANES : (i + 1) * LANES] = part[n].T
    grown_t = jnp.concatenate(part[:blocks], axis=1)
    for step in range(ITERS):
        inner = full_dot(grown_t, grown_t, 1, 1)
        if step < ITERS - 1:
            ready = right(full_dot(grown_t, gram[...], 1, 0), 0)
            grown_t = short_dot(left(inverse_lower(inner), 1), ready, 1, 0)
        else:
            rows = jnp.concatenate([fib[b].reshape(-1, LANES) for b in range(blocks)], axis=1)
            ready = left(jnp.concatenate([grown_t.T, full_dot(rows, grown_t, 1, 1)], axis=0), 1)
            both = short_dot(ready, right(inverse_lower(inner), 1), 1, 1)
            factor[...] = both[:width]
            core[...] = both[width:]


def on_device(sizes, field):
    nz, nx, ny = sizes
    steps, width_x, width_y, width_z = field.shape
    cells = width_y // ny
    width = width_z * ny
    planes = nx * ny
    rows = steps * width_x * cells
    pair_rows = len(block_pairs(ny)) * LANES
    half = pair_rows // 2
    piece = half // planes
    tiles = piece // 8
    f32 = jnp.float32
    dma = pltpu.SemaphoreType.DMA
    fib, sums = pl.pallas_call(
        functools.partial(gather_kernel, sizes, rows * nz * nx * 2 * ny),
        out_shape=(
            jax.ShapeDtypeStruct((ny, steps, width_x, cells, width_z), f32),
            jax.ShapeDtypeStruct((2, planes, piece, LANES), f32),
        ),
        in_specs=[pl.BlockSpec(memory_space=pl.ANY)],
        out_specs=(VMEM, VMEM),
        scratch_shapes=[
            pltpu.VMEM((pair_rows, LANES), f32),
            pltpu.VMEM((half, LANES), f32),
            pltpu.VMEM((half, LANES), f32),
            pltpu.VMEM((planes - 1, piece, LANES), f32),
            pltpu.VMEM((piece, LANES), f32),
            pltpu.VMEM((nz, 8, LANES), f32),
            pltpu.VMEM((tiles, 8, LANES), f32),
            pltpu.SemaphoreType.REGULAR((3,)),
            dma((2 * steps,)),
            dma,
            dma((2 * steps,)),
            dma,
            dma((nx // 2 + ny // 2 + 1,)),
            dma,
            dma,
            dma,
            dma,
            dma,
            dma((tiles,)),
            dma,
            dma((nx // 2 + ny // 2,)),
            dma,
            dma,
        ],
        compiler_params=pltpu.CompilerParams(
            collective_id=0, has_side_effects=True, vmem_limit_bytes=52 * 2**20
        ),
        name="gather_gram",
    )(field)
    core, factor = pl.pallas_call(
        factor_kernel,
        out_shape=(
            jax.ShapeDtypeStruct((rows, RANK), f32),
            jax.ShapeDtypeStruct((width, RANK), f32),
        ),
        in_specs=[VMEM, VMEM],
        out_specs=(VMEM, VMEM),
        scratch_shapes=[
            pltpu.VMEM((width, width), f32),
        ],
        compiler_params=pltpu.CompilerParams(vmem_limit_bytes=24 * 2**20),
        name="factor_core",
    )(fib, sums.reshape(pair_rows, LANES))
    return core.reshape(steps, width_x, cells, RANK), factor


def solution(mesh):
    sizes = (mesh.shape["gx"], mesh.shape["gy"] // 2, mesh.shape["gz"])
    return jax.shard_map(
        functools.partial(on_device, sizes),
        mesh=mesh,
        in_specs=(P(None, "gx", "gy", "gz"),),
        out_specs=(P(None, "gx", ("gy", "gz"), None), P()),
        check_vma=False,
    )
```

```python
import functools

import jax
import jax.numpy as jnp
from jax import lax
from jax.experimental import pallas as pl
from jax.experimental.pallas import tpu as pltpu
from jax.sharding import PartitionSpec as P

RANK = 128
ITERS = 4
LANES = 128
PANEL = 32
BLOCK = 16
VMEM = pl.BlockSpec(memory_space=pltpu.VMEM)


def full_dot(a, b, ca, cb):
    return lax.dot_general(
        a,
        b,
        (((ca,), (cb,)), ((), ())),
        precision=lax.Precision.HIGHEST,
        preferred_element_type=jnp.float32,
    )


def block_pairs(blocks):
    return [(i, j) for i in range(blocks) for j in range(i, blocks)]


def ring(n, k):
    return min(k % n, -k % n)


def gather_kernel(
    sizes, total_rows, field, fib, sums, acc, half, core_in, plane_in, mine, z_in, z_sum,
    known, own_sem, a2a_send, a2a_recv, core_send, core_recv, plane_send, plane_recv, z_send, z_recv,
    zg_send, zg_recv, pg_send, pg_recv, cg_send, cg_recv,
):
    nz, nx, ny = sizes
    planes = nx * ny
    blocks = ny
    pairs = block_pairs(blocks)
    cells = fib.shape[3]
    steps = fib.shape[1]
    half_rows = half.shape[0]
    piece = plane_in.shape[1]
    tiles = piece // 8
    z = lax.axis_index("gx")
    gy = lax.axis_index("gy")
    x = gy // 2
    c = gy % 2
    y = lax.axis_index("gz")
    p = x * ny + y

    def at_x(k):
        return {"gy": lax.rem(x + k % nx, nx) * 2 + c}

    def at_y(k):
        return {"gz": lax.rem(y + k % ny, ny)}

    def at_z(k):
        return {"gx": lax.rem(z + k % nz, nz)}

    other = {"gy": x * 2 + (1 - c)}

    def arrived(ref, sem):
        pltpu.make_async_remote_copy(
            src_ref=ref, dst_ref=ref, send_sem=sem, recv_sem=sem, device_id=other
        ).wait_recv()

    def left_here(ref, sem):
        pltpu.make_async_remote_copy(
            src_ref=ref, dst_ref=ref, send_sem=sem, recv_sem=sem, device_id=other
        ).wait_send()

    wide = fib.shape[2]
    cuts = [(s, 0, wide) for s in range(steps - 1)]
    cuts += [(steps - 1, 0, wide // 2), (steps - 1, wide // 2, wide // 4), (steps - 1, wide - wide // 4, wide // 4)]
    chunks = [(s, pl.ds(x0, deep)) for s, x0, deep in cuts]
    for n, (s, part) in enumerate(chunks):
        copy = pltpu.make_async_copy(
            field.at[s, part, pl.ds(y * cells, cells), :], fib.at[y, s, part], own_sem
        )
        copy.start()

    barrier = pltpu.get_barrier_semaphore()
    near = [at_y(k) for k in range(1, ny)] + [other, at_x(1), at_x(-1), at_z(1), at_z(-1)]
    for device in near:
        pl.semaphore_signal(barrier, inc=1, device_id=device)
    pl.semaphore_wait(barrier, len(near))

    order = sorted(range(1, ny), key=lambda k: ring(ny, k))
    for n, (s, part) in enumerate(chunks):
        for k in order:
            to = lax.rem(y + k, ny)
            copy = pltpu.make_async_remote_copy(
                src_ref=field.at[s, part, pl.ds(to * cells, cells), :],
                dst_ref=fib.at[y, s, part],
                send_sem=a2a_send,
                recv_sem=a2a_recv.at[n],
                device_id={"gz": to},
            )
            copy.start()
    rounds = [[at_x(1), at_x(-1), at_z(1), at_z(-1)], [at_z(2), at_z(-2)], [at_z(4), at_z(-4)]]
    if nx > 2:
        rounds[1].append(at_x(2))
    for i, devices in enumerate(rounds):
        for device in devices:
            pl.semaphore_signal(known.at[i], inc=1, device_id=device)
        pl.semaphore_wait(known.at[i], len(devices))

    for n, (s, part) in enumerate(chunks):
        if n == 0:
            pltpu.make_async_copy(fib.at[0], fib.at[0], own_sem).wait()
        arrived(fib.at[pl.ds(0, ny - 1), s, part], a2a_recv.at[n])
        x0, deep = cuts[n][1:]
        rows = jnp.concatenate([fib[b, s, x0 : x0 + deep].reshape(-1, LANES) for b in range(blocks)], axis=1)
        lhs, rhs = left(rows, 0), right(rows, 0)
        for i in range(0, blocks, 2):
            term = short_dot(lhs[:, i * LANES : (i + 2) * LANES], rhs[:, i * LANES :], 0, 0)
            for a in (0, 1):
                for b in range(i + a, blocks):
                    r = pairs.index((i + a, b)) * LANES
                    part = term[a * LANES : (a + 1) * LANES, (b - i) * LANES : (b - i + 1) * LANES]
                    if n == 0:
                        acc[r : r + LANES, :] = part
                    else:
                        acc[r : r + LANES, :] = acc[r : r + LANES, :] + part

    offsets = [(i, j) for i in range(nx) for j in range(ny) if (i, j) != (0, 0)]
    offsets.sort(key=lambda o: -(ring(nx, o[0]) + ring(ny, o[1])))

    def plane_at(i, j):
        to_x, to_y = lax.rem(x + i % nx, nx), lax.rem(y + j % ny, ny)
        return to_x * ny + to_y, {"gy": to_x * 2 + c, "gz": to_y}

    def rows_of(start, q):
        return pl.ds(pl.multiple_of(start + q * piece, 8), piece)

    hops = [ring(nx, i) + ring(ny, j) for i, j in offsets] + [0]
    groups = [[n for n in range(planes) if hops[n] == h] for h in range(max(hops), -1, -1)]
    keep = c * half_rows
    give = (1 - c) * half_rows
    for n, (i, j) in enumerate(offsets + [(0, 0)]):
        q = plane_at(i, j)[0]
        copy = pltpu.make_async_remote_copy(
            src_ref=acc.at[rows_of(give, q)],
            dst_ref=core_in.at[rows_of(0, q)],
            send_sem=core_send,
            recv_sem=core_recv.at[hops[0] - hops[n]],
            device_id=other,
        )
        copy.start()
    for n, (i, j) in enumerate(offsets):
        q, device = plane_at(i, j)
        h = hops[0] - hops[n]
        if n == groups[h][0]:
            arrived(core_in.at[pl.ds(0, len(groups[h]) * piece)], core_recv.at[h])
        half[rows_of(0, q), :] = acc[rows_of(keep, q), :] + core_in[rows_of(0, q), :]
        copy = pltpu.make_async_remote_copy(
            src_ref=half.at[rows_of(0, q)],
            dst_ref=plane_in.at[n],
            send_sem=plane_send,
            recv_sem=plane_recv,
            device_id=device,
        )
        copy.start()
    arrived(core_in.at[pl.ds(0, piece)], core_recv.at[len(groups) - 1])
    total = acc[rows_of(keep, p), :] + core_in[rows_of(0, p), :]
    arrived(plane_in, plane_recv)
    for n in range(len(offsets)):
        total = total + plane_in[n]
    mine[...] = total

    spread = nz // tiles
    keepers = [(t * spread % nz, (t * spread + nz // 2) % nz) for t in range(tiles)]
    assert len({v for pair in keepers for v in pair}) == 2 * tiles
    reach = sorted((k for k in range(1 - nz // 4, nz // 4 + 1) if k), key=lambda k: -ring(nz, k))
    keeps = [(z == a) | (z == b) for a, b in keepers]
    keeper = functools.reduce(lambda v, w: v | w, keeps)
    tile = sum(t * keeps[t].astype(jnp.int32) for t in range(tiles))

    def z_copy(t, m):
        return pltpu.make_async_remote_copy(
            src_ref=mine.at[pl.ds(t * 8, 8)],
            dst_ref=z_in.at[z],
            send_sem=z_send,
            recv_sem=z_recv,
            device_id={"gx": keepers[t][m]},
        )

    def zg_copy(i, t):
        return pltpu.make_async_remote_copy(
            src_ref=z_sum.at[t],
            dst_ref=z_sum.at[t],
            send_sem=zg_send,
            recv_sem=zg_recv.at[t],
            device_id=at_z(reach[i]),
        )

    for t in range(tiles):
        for m in (0, 1):

            @pl.when(z != keepers[t][m])
            def _():
                z_copy(t, m).start()

    @pl.when(keeper)
    def _():
        z_in[z] = mine[pl.ds(pl.multiple_of(tile * 8, 8), 8), :]
        arrived(z_in.at[pl.ds(0, nz - 1)], z_recv)
        total = z_in[0]
        for w in range(1, nz):
            total = total + z_in[w]
        z_sum[tile] = total * jnp.float32(1.0 / total_rows)
        for i in range(len(reach)):
            zg_copy(i, tile).start()

    for t in range(tiles):

        @pl.when(jnp.logical_not(keeps[t]))
        def _():
            zg_copy(0, t).wait_recv()

    sums[c, p] = z_sum[...].reshape(piece, LANES)

    def cg_copy(q):
        return pltpu.make_async_remote_copy(
            src_ref=sums.at[c, q],
            dst_ref=sums.at[c, q],
            send_sem=cg_send,
            recv_sem=cg_recv,
            device_id=other,
        )

    for n, (i, j) in enumerate(offsets):
        pltpu.make_async_remote_copy(
            src_ref=sums.at[c, p],
            dst_ref=sums.at[c, p],
            send_sem=pg_send,
            recv_sem=pg_recv.at[hops[0] - hops[n]],
            device_id=plane_at(i, j)[1],
        ).start()
    cg_copy(p).start()
    for h in reversed(range(len(groups) - 1)):
        arrived(sums.at[0, pl.ds(0, len(groups[h]))], pg_recv.at[h])
        for n in groups[h]:
            i, j = offsets[n]
            cg_copy(plane_at(-i, -j)[0]).start()

    left_here(fib.at[pl.ds(0, ny - 1)], a2a_send)
    left_here(acc.at[pl.ds(0, half_rows)], core_send)
    left_here(half.at[pl.ds(0, half_rows - piece)], plane_send)
    left_here(sums.at[0, pl.ds(0, planes - 1)], pg_send)

    @pl.when(keeper)
    def _():
        left_here(z_in.at[pl.ds(0, 2 * tiles - 1)], z_send)
        left_here(z_in.at[pl.ds(0, len(reach))], zg_send)

    @pl.when(jnp.logical_not(keeper))
    def _():
        left_here(z_in.at[pl.ds(0, 2 * tiles)], z_send)

    left_here(sums.at[0], cg_send)
    arrived(sums.at[0], cg_recv)


def reciprocal(d):
    r = pl.reciprocal(d, approx=True)
    return r * (2.0 - d * r)


def short_dot(a, b, ca, cb):
    return lax.dot_general(a, b, (((ca,), (cb,)), ((), ())), preferred_element_type=jnp.float32)


def split(v):
    high = v.astype(jnp.bfloat16)
    rest = v - high.astype(jnp.float32)
    middle = rest.astype(jnp.bfloat16)
    return high, middle, (rest - middle.astype(jnp.float32)).astype(jnp.bfloat16)


def left(v, axis):
    h, m, t = split(v)
    return jnp.concatenate([h, h, m, m, h, t], axis=axis)


def right(v, axis):
    h, m, t = split(v)
    return jnp.concatenate([h, m, h, m, t, h], axis=axis)


def row(v, i):
    return jnp.broadcast_to(v[i : i + 1, :], (8, v.shape[1]))


def inverse_lower(inner):
    rank = inner.shape[0]
    count, groups = rank // PANEL, PANEL // 8
    row8 = lax.broadcasted_iota(jnp.int32, (8, rank), 0)
    lane8 = lax.broadcasted_iota(jnp.int32, (8, rank), 1)
    row_of = lax.broadcasted_iota(jnp.int32, (PANEL, rank), 0)
    lane_of = lax.broadcasted_iota(jnp.int32, (PANEL, rank), 1)
    rest = [inner[t * PANEL : (t + 1) * PANEL] for t in range(count)]
    result = []
    for s in range(count):
        j0, j1 = s * PANEL, (s + 1) * PANEL
        panel = [rest[s][8 * g : 8 * g + 8, :] for g in range(groups)]
        done = {}
        for g0 in range(0, groups, BLOCK // 8):
            c0 = j0 + 8 * g0
            cols = {}
            for k in range(BLOCK):
                for g in range(g0 + k // 8, groups):
                    cols[k, g] = jnp.broadcast_to(panel[g][:, c0 + k : c0 + k + 1], (8, rank))

            def at(j, k):
                return row(cols[j, g0 + k // 8], k % 8)

            p, q, r = at(0, 0), at(0, 1), at(1, 1)
            for j in range(0, BLOCK, 2):
                gj, ij = g0 + j // 8, j % 8
                column = c0 + j
                det = p * r - q * q
                inv = reciprocal(det)
                following = None
                if j + 2 < BLOCK:
                    k = j + 2
                    u1, u2, v1, v2 = at(j, k), at(j + 1, k), at(j, k + 1), at(j + 1, k + 1)
                    a1, a2 = r * u1 - q * u2, p * u2 - q * u1
                    e1, e2 = r * v1 - q * v2, p * v2 - q * v1
                    following = (
                        at(k, k) - (a1 * u1 + a2 * u2) * inv,
                        at(k, k + 1) - (a1 * v1 + a2 * v2) * inv,
                        at(k + 1, k + 1) - (e1 * v1 + e2 * v2) * inv,
                    )
                pi, qi, ri = p * inv, q * inv, r * inv
                first = gj + 1 if ij == 6 else gj
                m1 = {g: cols[j, g] * ri - cols[j + 1, g] * qi for g in range(first, groups)}
                m2 = {g: cols[j + 1, g] * pi - cols[j, g] * qi for g in range(first, groups)}
                for k in range(j + 2, BLOCK):
                    w1, w2 = at(j, k), at(j + 1, k)
                    for g in range(g0 + k // 8, groups):
                        cols[k, g] = cols[k, g] - (m1[g] * w1 + m2[g] * w2)
                here = lane8 // 2 == column // 2
                row1 = jnp.where(here, jnp.where(lane8 == column, 1.0, 0.0), row(panel[gj], ij))
                row2 = jnp.where(here, jnp.where(lane8 == column, 0.0, 1.0), row(panel[gj], ij + 1))
                inv_p = reciprocal(p)
                done[8 * gj + ij] = row1 * lax.rsqrt(p)
                done[8 * gj + ij + 1] = (row2 - (q * inv_p) * row1) * lax.rsqrt(det * inv_p)
                for g in range(first, groups):
                    panel[g] = jnp.where(here, 0.0, panel[g]) - (m1[g] * row1 + m2[g] * row2)
                if following:
                    p, q, r = following
        upper = []
        for g in range(groups):
            v = done[8 * g]
            for i in range(1, 8):
                v = jnp.where(row8 == i, done[8 * g + i], v)
            upper.append(v)
        upper = jnp.concatenate(upper, axis=0)
        lower = lane_of <= row_of + j0
        result.append(jnp.where(lower, upper, 0.0))
        if s + 1 < count:
            kept = jnp.where(lower | (lane_of >= j1), upper, 0.0)
            change = short_dot(left(upper, 0)[:, j1:], right(kept, 0), 0, 0)
            block = (lane_of >= j0) & (lane_of < j1)
            for t in range(s + 1, count):
                part = change[(t - s - 1) * PANEL : (t - s) * PANEL]
                rest[t] = jnp.where(block, 0.0, rest[t]) - part
    return jnp.concatenate(result, axis=0)


def factor_kernel(fib, sums, core, factor, gram):
    blocks = fib.shape[0]
    width = blocks * LANES
    pairs = block_pairs(blocks)
    part = [sums[n * LANES : (n + 1) * LANES, :] for n in range(len(pairs))]
    for n, (i, j) in enumerate(pairs):
        gram[i * LANES : (i + 1) * LANES, j * LANES : (j + 1) * LANES] = part[n]
        if i != j:
            gram[j * LANES : (j + 1) * LANES, i * LANES : (i + 1) * LANES] = part[n].T
    grown_t = jnp.concatenate(part[:blocks], axis=1)
    for step in range(ITERS):
        inner = full_dot(grown_t, grown_t, 1, 1)
        if step < ITERS - 1:
            ready = right(full_dot(grown_t, gram[...], 1, 0), 0)
            grown_t = short_dot(left(inverse_lower(inner), 1), ready, 1, 0)
        else:
            rows = jnp.concatenate([fib[b].reshape(-1, LANES) for b in range(blocks)], axis=1)
            ready = left(jnp.concatenate([grown_t.T, full_dot(rows, grown_t, 1, 1)], axis=0), 1)
            both = short_dot(ready, right(inverse_lower(inner), 1), 1, 1)
            factor[...] = both[:width]
            core[...] = both[width:]


def on_device(sizes, field):
    nz, nx, ny = sizes
    steps, width_x, width_y, width_z = field.shape
    cells = width_y // ny
    width = width_z * ny
    planes = nx * ny
    rows = steps * width_x * cells
    pair_rows = len(block_pairs(ny)) * LANES
    half = pair_rows // 2
    piece = half // planes
    tiles = piece // 8
    f32 = jnp.float32
    dma = pltpu.SemaphoreType.DMA
    fib, sums = pl.pallas_call(
        functools.partial(gather_kernel, sizes, rows * nz * nx * 2 * ny),
        out_shape=(
            jax.ShapeDtypeStruct((ny, steps, width_x, cells, width_z), f32),
            jax.ShapeDtypeStruct((2, planes, piece, LANES), f32),
        ),
        in_specs=[pl.BlockSpec(memory_space=pl.ANY)],
        out_specs=(VMEM, VMEM),
        scratch_shapes=[
            pltpu.VMEM((pair_rows, LANES), f32),
            pltpu.VMEM((half, LANES), f32),
            pltpu.VMEM((half, LANES), f32),
            pltpu.VMEM((planes - 1, piece, LANES), f32),
            pltpu.VMEM((piece, LANES), f32),
            pltpu.VMEM((nz, 8, LANES), f32),
            pltpu.VMEM((tiles, 8, LANES), f32),
            pltpu.SemaphoreType.REGULAR((3,)),
            dma,
            dma,
            dma((steps + 2,)),
            dma,
            dma((nx // 2 + ny // 2 + 1,)),
            dma,
            dma,
            dma,
            dma,
            dma,
            dma((tiles,)),
            dma,
            dma((nx // 2 + ny // 2,)),
            dma,
            dma,
        ],
        compiler_params=pltpu.CompilerParams(
            collective_id=0, has_side_effects=True, vmem_limit_bytes=52 * 2**20
        ),
        name="gather_gram",
    )(field)
    core, factor = pl.pallas_call(
        factor_kernel,
        out_shape=(
            jax.ShapeDtypeStruct((rows, RANK), f32),
            jax.ShapeDtypeStruct((width, RANK), f32),
        ),
        in_specs=[VMEM, VMEM],
        out_specs=(VMEM, VMEM),
        scratch_shapes=[
            pltpu.VMEM((width, width), f32),
        ],
        compiler_params=pltpu.CompilerParams(vmem_limit_bytes=24 * 2**20),
        name="factor_core",
    )(fib, sums.reshape(pair_rows, LANES))
    return core.reshape(steps, width_x, cells, RANK), factor


def solution(mesh):
    sizes = (mesh.shape["gx"], mesh.shape["gy"] // 2, mesh.shape["gz"])
    return jax.shard_map(
        functools.partial(on_device, sizes),
        mesh=mesh,
        in_specs=(P(None, "gx", "gy", "gz"),),
        out_specs=(P(None, "gx", ("gy", "gz"), None), P()),
        check_vma=False,
    )
```
